32 devices in a mesh: ctx: 16 (over z, x, core), tp: 2 (over y).
Axes of the slice: x: 2, y: 2, z: 4, core: 2. Of those that a mesh axis runs over, the one named last changes fastest.
Arguments:
- queries: bfloat16 [2048, 4096], P('ctx', 'tp'), may hold values from -6 to 6
- keys: bfloat16 [2048, 8192], P('ctx', 'tp'), may hold values from -6 to 6
- values: bfloat16 [2048, 8192], P('ctx', 'tp'), may hold values from -6 to 6
- beta_logit: float32 [32, 4096], P('tp', 'ctx'), may hold values from -8 to 8
- out_weight: bfloat16 [4096, 4096], P('ctx', 'tp'), may hold values from -0.125 to 0.125
- out_grad: bfloat16 [2048, 4096], P('ctx', 'tp'), may hold values from -6 to 6
Outputs:
- mixed: bfloat16 [2048, 4096], P('ctx', 'tp')
- query_grad: bfloat16 [2048, 4096], P('ctx', 'tp')
- key_grad: bfloat16 [2048, 8192], P('ctx', 'tp')
- value_grad: bfloat16 [2048, 8192], P('ctx', 'tp')
- logit_grad: float32 [32, 4096], P('tp', 'ctx')
- weight_grad: float32 [4096, 4096], P('ctx', 'tp')
The draws below stay inside these ranges and needn't reach their ends.
All inputs are finite; a program needn't handle non-finite values.
Results may differ from the reference program's by a relative error of at most 0.023.
Values may be sent and summed in bfloat16 or wider, within the bound.
A program may use at most 128 MiB of HBM per device.

```python
import math
import jax
import jax.numpy as jnp
from jax import lax

D = 4096
HEADS = 32
DK = 128
L_DEV = 128
HV = 4096
SEQ = 2048
N_CTX = 16


def draw_beta_logit(key, part):
    key_centre = jax.random.fold_in(key, 11)
    key_noise = jax.random.fold_in(key, 12)
    centre = jax.random.uniform(key_centre, (HEADS, 1), jnp.float32, -2.5, 2.5)
    noise = jax.random.normal(key_noise, (HEADS, 2 * SEQ), jnp.float32)
    return jnp.clip(centre + noise, -8.0, 8.0).astype(jnp.float32)


def strengthened(values, own_key, source, target, parts, factor):
    owner, partner = [(jnp.arange(values.shape[axis_at]) // (values.shape[axis_at] // parts)).reshape([-1 if axis == axis_at else 1 for axis in range(values.ndim)]) for axis_at in (source, target)]
    chosen = jax.random.permutation(own_key, parts)[partner]
    strong = (owner == chosen) | (owner == (partner + parts // 2) % parts)
    return jnp.where(strong, factor * values, values)


def levels(rng, extent, split, low, top_value):
    gain = 1.0
    for dim, parts in split:
        draws = jax.random.uniform(jax.random.fold_in(jax.random.fold_in(rng, 6), dim), (parts,), jnp.float32, low / len(split), top_value / len(split))
        gain = gain * jnp.repeat(jnp.exp(draws), extent[dim] // parts).reshape((-1,) + (1,) * (len(extent) - 1 - dim))
    return gain


def gaussian(stream_key, extent, scale, most, cuts=(), held_as=jnp.bfloat16):
    values = scale * jax.random.normal(stream_key, extent, jnp.float32)
    if cuts:
        values = values * levels(stream_key, extent, cuts, -0.22, 0.18)
    return jnp.clip(values, -most, most).astype(held_as)


def bell_draw_with(key, shape, scale, bound, cuts, heavy, held_as=jnp.bfloat16):
    array = scale * jax.random.normal(key, shape, jnp.float32)
    if cuts:
        array = array * levels(key, shape, cuts, -0.22, 0.18)
    return jnp.clip(strengthened(array, jax.random.fold_in(key, 3), *heavy), -bound, bound).astype(held_as)


def setup_inputs(seed: int = 0) -> dict:
    splits = jax.random.split(jax.random.key(seed), 7)
    queries = gaussian(splits[0], (SEQ, HV), 1.0, 6.0, ((0, 16), (1, 2)))
    keys = gaussian(splits[1], (SEQ, 2 * HV), 1.0, 6.0, ((0, 16), (1, 2)))
    values = gaussian(splits[2], (SEQ, 2 * HV), 1.0, 6.0, ((0, 16), (1, 2)))
    beta_logit = draw_beta_logit(jax.random.fold_in(splits[6], 71), 0)
    out_weight = bell_draw_with(splits[4], (D, HV), HV ** -0.5, 0.125, ((0, 16), (1, 2)), (1, 0, 16, 2.0))
    out_grad = bell_draw_with(splits[5], (SEQ, D), 1.0, 6.0, ((0, 16), (1, 2)), (0, 1, 16, 2.0))
    return {"queries": queries, "keys": keys, "values": values, "beta_logit": beta_logit, "out_weight": out_weight, "out_grad": out_grad}


def normalize(matrix):
    return matrix * lax.rsqrt(lax.optimization_barrier(jnp.sum(matrix * matrix, axis=-1, keepdims=True)) + 1e-06)

def mix_blocks(memory, query_heads, key_heads, value_heads, strength):
    head_count, length, width = query_heads.shape
    blocks = length // 64
    query_blk = query_heads.reshape(head_count, blocks, 64, width).transpose(1, 0, 2, 3)
    key_blk = key_heads.reshape(head_count, blocks, 128, width).transpose(1, 0, 2, 3)
    value_blk = value_heads.reshape(head_count, blocks, 128, value_heads.shape[2]).transpose(1, 0, 2, 3)
    gate_blk = strength.reshape(head_count, blocks, 128).transpose(1, 0, 2)
    row_ids = lax.broadcasted_iota(jnp.int32, (128, 128), 0)
    col_ids = lax.broadcasted_iota(jnp.int32, (128, 128), 1)
    below_diag = col_ids < row_ids
    token_ids = lax.broadcasted_iota(jnp.int32, (64, 128), 0)
    refl_ids = lax.broadcasted_iota(jnp.int32, (64, 128), 1)
    visible = refl_ids <= 2 * token_ids + 1
    identity_map = jnp.eye(128, dtype=jnp.float32)
    highest = lax.Precision.HIGHEST

    def advance(current, pieces):
        query_x, key_x, value_x, gate_x = pieces
        key_gram = jnp.einsum('hid,hjd->hij', key_x, key_x, precision=highest)
        system = identity_map + jnp.where(below_diag, gate_x[:, :, None] * key_gram, 0.0)
        right_side = gate_x[:, :, None] * (value_x - jnp.einsum('hid,hde->hie', key_x, current, precision=highest))
        updates = lax.linalg.triangular_solve(system, right_side, left_side=True, lower=True, unit_diagonal=True)
        scores = jnp.where(visible, jnp.einsum('htd,hid->hti', query_x, key_x, precision=highest), 0.0)
        result = jnp.einsum('htd,hde->hte', query_x, current, precision=highest)
        result = result + jnp.einsum('hti,hie->hte', scores, updates, precision=highest)
        current = current + jnp.einsum('hid,hie->hde', key_x, updates, precision=highest)
        return (current, result)
    memory, block_out = lax.scan(advance, memory, (query_blk, key_blk, value_blk, gate_blk))
    block_out = block_out.transpose(1, 0, 2, 3).reshape(head_count, length, block_out.shape[3])
    return (block_out, memory)

def group_map(memory, query_f, key_f, value_f, logits):
    head_count = logits.shape[0]
    length = query_f.shape[0]
    width = query_f.shape[1] // head_count
    query_heads = normalize(query_f.reshape(length, head_count, width)).transpose(1, 0, 2)
    key_heads = normalize(key_f.reshape(length, head_count, 2, width)).transpose(1, 0, 2, 3).reshape(head_count, 2 * length, width)
    value_heads = value_f.reshape(length, head_count, 2, width).transpose(1, 0, 2, 3).reshape(head_count, 2 * length, width)
    strength = 2.0 * jax.nn.sigmoid(logits)
    block_out, memory = mix_blocks(memory, query_heads, key_heads, value_heads, strength)
    return (block_out.transpose(1, 0, 2).reshape(length, head_count * width), memory)

def reference(queries, keys, values, beta_logit, out_weight, out_grad):
    query_f = queries.astype(jnp.float32)
    key_f = keys.astype(jnp.float32)
    value_f = values.astype(jnp.float32)
    start_state = jnp.zeros((HEADS, DK, DK), jnp.float32)

    def forward(query_in, key_in, value_in, logit_in):
        return group_map(start_state, query_in, key_in, value_in, logit_in)[0]
    heads_f, pull = jax.vjp(forward, query_f, key_f, value_f, beta_logit)
    heads_out = heads_f.astype(jnp.bfloat16)
    mixed = jnp.dot(heads_out.astype(jnp.float32), out_weight.T.astype(jnp.float32), preferred_element_type=jnp.float32).astype(jnp.bfloat16)
    head_grad = jnp.dot(out_grad.astype(jnp.float32), out_weight.astype(jnp.float32), preferred_element_type=jnp.float32)
    query_grad, key_grad, value_grad, logit_grad = pull(head_grad)
    scale_factor = 1.0 / math.sqrt(SEQ)

    def accumulate(total, pieces):
        grad_blk, heads_blk = pieces
        partial_term = jnp.dot(grad_blk.T.astype(jnp.float32), heads_blk.astype(jnp.float32), preferred_element_type=jnp.float32) * scale_factor
        partial_term = lax.optimization_barrier(partial_term.astype(jnp.bfloat16)).astype(jnp.float32)
        return (total + partial_term, None)
    weight_grad, _ = lax.scan(accumulate, jnp.zeros((D, HV), jnp.float32), (out_grad.reshape(N_CTX, L_DEV, D), heads_out.reshape(N_CTX, L_DEV, HV)))
    return (mixed, query_grad.astype(jnp.bfloat16), key_grad.astype(jnp.bfloat16), value_grad.astype(jnp.bfloat16), logit_grad, weight_grad)
```

```python
import functools
import math

import jax
import jax.numpy as jnp
from jax import lax
from jax.experimental import pallas as pl
from jax.experimental.pallas import tpu as pltpu
from jax.sharding import PartitionSpec as P

F32 = jnp.float32
BF16 = jnp.bfloat16
NN = (((1,), (0,)), ((), ()))
NT = (((1,), (1,)), ((), ()))
TN = (((0,), (0,)), ((), ()))
LIMIT = 56 * 1024 * 1024


def halves(x):
    high = x.astype(BF16)
    return (high, (x - high.astype(F32)).astype(BF16))


def mm(left, right, dims=NN):
    total = None
    for i, a in enumerate(left):
        for j, b in enumerate(right):
            if i + j < 2:
                term = lax.dot_general(a, b, dims, preferred_element_type=F32)
                total = term if total is None else total + term
    return total


def inverse_norm(x):
    return lax.rsqrt(jnp.sum(x * x, axis=-1, keepdims=True) + 1e-06)


def stacked(ref, head, width):
    start = head * 2 * width
    return jnp.concatenate(
        [ref[:, start : start + width], ref[:, start + width : start + 2 * width]], axis=0
    )


def time_ids(length, axis):
    ids = lax.broadcasted_iota(jnp.int32, (2 * length, 2 * length), axis)
    second = (ids >= length).astype(jnp.int32)
    return 2 * (ids - second * length) + second


def visible_mask(length):
    token = lax.broadcasted_iota(jnp.int32, (length, 2 * length), 0)
    refl = lax.broadcasted_iota(jnp.int32, (length, 2 * length), 1)
    refl = jnp.where(refl >= length, refl - length, refl)
    return refl <= token


def prepare_kernel(group, q_ref, k_ref, v_ref, b_ref, th_ref, tl_ref, wu_ref, m_ref, off_ref, qe_ref, o0_ref):
    length, width = q_ref.shape[0], q_ref.shape[1] // group
    rows, cols = time_ids(length, 0), time_ids(length, 1)
    visible = visible_mask(length)
    diff = rows ^ cols
    eye = (rows == cols).astype(F32)
    small_eye = (
        lax.broadcasted_iota(jnp.int32, (width, width), 0)
        == lax.broadcasted_iota(jnp.int32, (width, width), 1)
    ).astype(F32)
    state = []
    for g in range(group):
        key = stacked(k_ref, g, width).astype(F32)
        value = stacked(v_ref, g, width).astype(F32)
        query = q_ref[:, g * width : (g + 1) * width].astype(F32)
        key = key * inverse_norm(key)
        query = query * inverse_norm(query)
        b = b_ref[g]
        kp, qp = halves(key), halves(query)
        system = jnp.where(cols < rows, b * mm(kp, kp, NT), 0.0)
        ah, al = halves(system)
        inv = eye - jnp.where(diff == 1, system, 0.0)
        state.append([kp, qp, ah, al, inv, key, query, value, b])
    step = 2
    while step < 2 * length:
        inside = (diff >= step) & (diff < 2 * step)
        for s in state:
            part = (
                jnp.where(inside, s[2], jnp.zeros_like(s[2])),
                jnp.where(inside, s[3], jnp.zeros_like(s[3])),
            )
            ip = halves(s[4])
            s[4] = s[4] - mm(ip, halves(mm(part, ip)))
        step *= 2
    for g, (kp, qp, _, _, inv, key, query, value, b) in enumerate(state):
        ip = halves(inv)
        th_ref[g] = ip[0]
        tl_ref[g] = ip[1]
        wu = mm(ip, halves(b * jnp.concatenate([key, value], axis=1)))
        wu_ref[g] = wu
        wup = halves(wu)
        ku = mm(kp, wup, TN)
        m_hi, m_lo = halves(small_eye - ku[:, :width])
        m_ref[g, 0] = m_hi
        m_ref[g, 1] = m_lo
        off_ref[g] = ku[:, width:]
        scores = jnp.where(visible, mm(qp, kp, NT), 0.0)
        pu = mm(halves(scores), wup)
        q_hi, q_lo = halves(query - pu[:, :width])
        qe_ref[g, 0] = q_hi
        qe_ref[g, 1] = q_lo
        o0_ref[g] = pu[:, width:]


def chain_barrier(me, n):
    barrier = pltpu.get_barrier_semaphore()
    for other in (lax.rem(me + 1, n), lax.rem(me + n - 1, n)):
        pl.semaphore_signal(
            barrier, inc=1, device_id={"ctx": other}, device_id_type=pl.DeviceIdType.MESH
        )
    pl.semaphore_wait(barrier, 2)


def chain(n, place, way, heads, held, out, send_sem, recv_sem, advance):
    me = lax.axis_index("ctx")
    other = lax.rem(me + way + n, n)

    @pl.when(place == 0)
    def _():
        held[...] = jnp.zeros_like(held)

    def move(h):
        return pltpu.make_async_remote_copy(
            src_ref=out.at[h],
            dst_ref=held.at[h],
            send_sem=send_sem.at[h],
            recv_sem=recv_sem.at[h],
            device_id={"ctx": other},
            device_id_type=pl.DeviceIdType.MESH,
        )

    def step(h, carry):
        @pl.when(place > 0)
        def _():
            move(h).wait_recv()

        @pl.when(place < n - 1)
        def _():
            out[h] = advance(h, held[h]).astype(BF16)
            move(h).start()

        return carry

    lax.fori_loop(0, heads, step, 0)

    @pl.when(place < n - 1)
    def _():
        def finish(h, carry):
            move(h).wait_send()
            return carry

        lax.fori_loop(0, heads, finish, 0)


def forward_kernel(n, m_ref, off_ref, qe_ref, o0_ref, s_ref, ho_ref, held, out, send_sem, recv_sem):
    heads, width = off_ref.shape[0], off_ref.shape[1]
    me = lax.axis_index("ctx")
    chain_barrier(me, n)

    def advance(h, state):
        return mm((m_ref[h, 0], m_ref[h, 1]), (state,)) + off_ref[h]

    chain(n, me, 1, heads, held, out, send_sem, recv_sem, advance)
    s_ref[...] = held[...]
    for h in range(heads):
        ho_ref[:, h * width : (h + 1) * width] = (
            mm((qe_ref[h, 0], qe_ref[h, 1]), (held[h],)) + o0_ref[h]
        ).astype(BF16)


def backward_kernel(n, m_ref, qe_ref, do_ref, d_ref, own, held, out, send_sem, recv_sem):
    heads, width = m_ref.shape[0], m_ref.shape[2]
    me = lax.axis_index("ctx")
    chain_barrier(me, n)
    for h in range(heads):
        own[h] = mm(
            (qe_ref[h, 0], qe_ref[h, 1]), halves(do_ref[:, h * width : (h + 1) * width]), TN
        )

    def advance(h, state):
        return mm((m_ref[h, 0], m_ref[h, 1]), (state,), TN) + own[h]

    chain(n, n - 1 - me, -1, heads, held, out, send_sem, recv_sem, advance)
    d_ref[...] = held[...]


def finish_kernel(group, q_ref, k_ref, v_ref, b_ref, th_ref, tl_ref, wu_ref, s_ref, d_ref, do_ref, dq_ref, dk_ref, dv_ref, db_ref):
    length, width = q_ref.shape[0], q_ref.shape[1] // group
    rows, cols = time_ids(length, 0), time_ids(length, 1)
    visible = visible_mask(length)
    below = cols < rows
    for g in range(group):
        here = slice(g * width, (g + 1) * width)
        key = stacked(k_ref, g, width).astype(F32)
        value = stacked(v_ref, g, width).astype(F32)
        query = q_ref[:, here].astype(F32)
        k_norm, q_norm = inverse_norm(key), inverse_norm(query)
        key, query = key * k_norm, query * q_norm
        b = b_ref[g]
        kp, qp = halves(key), halves(query)
        start, end_grad = (s_ref[g],), (d_ref[g],)
        gp = halves(do_ref[:, here])
        gram = mm(kp, kp, NT)
        scores = jnp.where(visible, mm(qp, kp, NT), 0.0)
        wu = wu_ref[g]
        updates = wu[:, width:] - mm(halves(wu[:, :width]), start)
        up = halves(updates)
        update_grad = mm(halves(scores), gp, TN) + mm(kp, end_grad)
        right_grad = mm((th_ref[g], tl_ref[g]), halves(update_grad), TN)
        score_grad = halves(jnp.where(visible, mm(gp, up, NT), 0.0))
        query_grad = mm(gp, start, NT) + mm(score_grad, kp)
        system_grad = jnp.where(below, -mm(halves(right_grad), up, NT), 0.0)
        residual = value - mm(kp, start)
        db_ref[g] = jnp.sum(right_grad * residual, axis=1, keepdims=True) + jnp.sum(
            system_grad * gram, axis=1, keepdims=True
        )
        gram_grad = halves(b * system_grad)
        value_grad = b * right_grad
        key_grad = (
            mm(score_grad, qp, TN)
            + mm(up, end_grad, NT)
            - mm(halves(value_grad), start, NT)
            + mm(gram_grad, kp)
            + mm(gram_grad, kp, TN)
        )
        query_grad = q_norm * (
            query_grad - query * jnp.sum(query * query_grad, axis=1, keepdims=True)
        )
        key_grad = k_norm * (key_grad - key * jnp.sum(key * key_grad, axis=1, keepdims=True))
        dq_ref[:, here] = query_grad.astype(BF16)
        for j in range(2):
            there = slice((2 * g + j) * width, (2 * g + j + 1) * width)
            dk_ref[:, there] = key_grad[j * length : (j + 1) * length].astype(BF16)
            dv_ref[:, there] = value_grad[j * length : (j + 1) * length].astype(BF16)


def per_head(group, *shape):
    return pl.BlockSpec((group,) + shape, lambda i: (i,) + (0,) * len(shape))


def per_column(group, length, width):
    return pl.BlockSpec((length, group * width), lambda i: (0, i))


def local(n, queries, keys, values, beta_logit, out_weight, out_grad):
    heads = beta_logit.shape[0]
    length = queries.shape[0]
    width = queries.shape[1] // heads
    double = 2 * length
    group = 2
    params = pltpu.CompilerParams(vmem_limit_bytes=LIMIT)

    weight_full = lax.all_gather(out_weight, "ctx", axis=0, tiled=True)
    grad_full = lax.all_gather(out_grad, "tp", axis=1, tiled=True)
    grad_cols = lax.all_to_all(grad_full, "ctx", split_axis=1, concat_axis=0, tiled=True)

    strength = 2.0 * jax.nn.sigmoid(beta_logit)
    gate = strength.reshape(heads, length, 2).transpose(0, 2, 1).reshape(heads, double, 1)

    shape = jax.ShapeDtypeStruct
    q_spec, k_spec = per_column(group, length, width), per_column(group, length, 2 * width)
    b_spec = per_head(group, double, 1)
    t_spec = per_head(group, double, double)
    wu_spec = per_head(group, double, 2 * width)
    inv_hi, inv_lo, wu, trans, offset, query_eff, own_out = pl.pallas_call(
        functools.partial(prepare_kernel, group),
        grid=(heads // group,),
        in_specs=[q_spec, k_spec, k_spec, b_spec],
        out_specs=[
            t_spec,
            t_spec,
            wu_spec,
            per_head(group, 2, width, width),
            per_head(group, width, width),
            per_head(group, 2, length, width),
            per_head(group, length, width),
        ],
        out_shape=[
            shape((heads, double, double), BF16),
            shape((heads, double, double), BF16),
            shape((heads, double, 2 * width), F32),
            shape((heads, 2, width, width), BF16),
            shape((heads, width, width), F32),
            shape((heads, 2, length, width), BF16),
            shape((heads, length, width), F32),
        ],
        compiler_params=params,
        name="prepare",
    )(queries, keys, values, gate)

    whole = pl.BlockSpec(memory_space=pltpu.VMEM)
    carried = [
        pltpu.VMEM((heads, width, width), BF16),
        pltpu.VMEM((heads, width, width), BF16),
        pltpu.SemaphoreType.DMA((heads,)),
        pltpu.SemaphoreType.DMA((heads,)),
    ]
    state_in, heads_out = pl.pallas_call(
        functools.partial(forward_kernel, n),
        in_specs=[whole] * 4,
        out_specs=[whole, whole],
        out_shape=[shape((heads, width, width), BF16), shape(queries.shape, BF16)],
        scratch_shapes=carried,
        compiler_params=pltpu.CompilerParams(
            vmem_limit_bytes=LIMIT, collective_id=0, has_side_effects=True
        ),
        name="forward_chain",
    )(trans, offset, query_eff, own_out)

    heads_full = lax.all_gather(heads_out, "ctx", axis=0, tiled=True)
    head_grad = jnp.dot(grad_full, weight_full, preferred_element_type=F32)

    state_grad = pl.pallas_call(
        functools.partial(backward_kernel, n),
        in_specs=[whole] * 3,
        out_specs=whole,
        out_shape=shape((heads, width, width), BF16),
        scratch_shapes=[pltpu.VMEM((heads, width, width), F32)] + carried,
        compiler_params=pltpu.CompilerParams(
            vmem_limit_bytes=LIMIT, collective_id=1, has_side_effects=True
        ),
        name="backward_chain",
    )(trans, query_eff, head_grad)

    mixed_cols = lax.psum_scatter(
        lax.dot_general(weight_full, heads_out, NT, preferred_element_type=F32).astype(BF16),
        "tp",
        scatter_dimension=0,
        tiled=True,
    )
    mixed = mixed_cols.T

    d_spec = per_head(group, width, width)
    query_grad, key_grad, value_grad, gate_grad = pl.pallas_call(
        functools.partial(finish_kernel, group),
        grid=(heads // group,),
        in_specs=[q_spec, k_spec, k_spec, b_spec, t_spec, t_spec, wu_spec, d_spec, d_spec, q_spec],
        out_specs=[q_spec, k_spec, k_spec, b_spec],
        out_shape=[
            shape(queries.shape, BF16),
            shape(keys.shape, BF16),
            shape(values.shape, BF16),
            shape((heads, double, 1), F32),
        ],
        compiler_params=params,
        name="finish",
    )(queries, keys, values, gate, inv_hi, inv_lo, wu, state_in, state_grad, head_grad)

    gate_grad = gate_grad.reshape(heads, 2, length).transpose(0, 2, 1).reshape(heads, double)
    logit_grad = gate_grad * strength * jax.nn.sigmoid(-beta_logit)

    scale_factor = 1.0 / math.sqrt(length * n)
    weight_grad = scale_factor * lax.dot_general(
        grad_cols, heads_full, TN, preferred_element_type=F32
    )
    return (mixed, query_grad, key_grad, value_grad, logit_grad, weight_grad)


def solution(mesh):
    placed = (
        P("ctx", "tp"),
        P("ctx", "tp"),
        P("ctx", "tp"),
        P("tp", "ctx"),
        P("ctx", "tp"),
        P("ctx", "tp"),
    )
    return jax.shard_map(
        functools.partial(local, mesh.shape["ctx"]),
        mesh=mesh,
        in_specs=placed,
        out_specs=(
            P("ctx", "tp"),
            P("ctx", "tp"),
            P("ctx", "tp"),
            P("ctx", "tp"),
            P("tp", "ctx"),
            P("ctx", "tp"),
        ),
        check_vma=False,
    )
```

```python
import functools
import math

import jax
import jax.numpy as jnp
from jax import lax
from jax.experimental import pallas as pl
from jax.experimental.pallas import tpu as pltpu
from jax.sharding import PartitionSpec as P

F32 = jnp.float32
BF16 = jnp.bfloat16
NN = (((1,), (0,)), ((), ()))
NT = (((1,), (1,)), ((), ()))
TN = (((0,), (0,)), ((), ()))
LIMIT = 56 * 1024 * 1024


def halves(x):
    high = x.astype(BF16)
    return (high, (x - high.astype(F32)).astype(BF16))


def mm(left, right, dims=NN):
    total = None
    for i, a in enumerate(left):
        for j, b in enumerate(right):
            if i + j < 2:
                term = lax.dot_general(a, b, dims, preferred_element_type=F32)
                total = term if total is None else total + term
    return total


def inverse_norm(x):
    return lax.rsqrt(jnp.sum(x * x, axis=-1, keepdims=True) + 1e-06)


def stacked(ref, head, width):
    start = head * 2 * width
    return jnp.concatenate(
        [ref[:, start : start + width], ref[:, start + width : start + 2 * width]], axis=0
    )


def time_ids(length, axis):
    ids = lax.broadcasted_iota(jnp.int32, (2 * length, 2 * length), axis)
    second = (ids >= length).astype(jnp.int32)
    return 2 * (ids - second * length) + second


def visible_mask(length):
    token = lax.broadcasted_iota(jnp.int32, (length, 2 * length), 0)
    refl = lax.broadcasted_iota(jnp.int32, (length, 2 * length), 1)
    refl = jnp.where(refl >= length, refl - length, refl)
    return refl <= token


def prepare_kernel(group, q_ref, k_ref, v_ref, b_ref, th_ref, tl_ref, wu_ref, m_ref, off_ref, qe_ref, o0_ref):
    length, width = q_ref.shape[0], q_ref.shape[1] // group
    rows, cols = time_ids(length, 0), time_ids(length, 1)
    visible = visible_mask(length)
    diff = rows ^ cols
    eye = (rows == cols).astype(F32)
    small_eye = (
        lax.broadcasted_iota(jnp.int32, (width, width), 0)
        == lax.broadcasted_iota(jnp.int32, (width, width), 1)
    ).astype(F32)
    state = []
    for g in range(group):
        key = stacked(k_ref, g, width).astype(F32)
        value = stacked(v_ref, g, width).astype(F32)
        query = q_ref[:, g * width : (g + 1) * width].astype(F32)
        key = key * inverse_norm(key)
        query = query * inverse_norm(query)
        b = b_ref[g]
        kp, qp = halves(key), halves(query)
        system = jnp.where(cols < rows, b * mm(kp, kp, NT), 0.0)
        ah, al = halves(system)
        inv = eye - jnp.where(diff == 1, system, 0.0)
        state.append([kp, qp, ah, al, inv, key, query, value, b])
    step = 2
    while step < 2 * length:
        inside = (diff >= step) & (diff < 2 * step)
        for s in state:
            part = (
                jnp.where(inside, s[2], jnp.zeros_like(s[2])),
                jnp.where(inside, s[3], jnp.zeros_like(s[3])),
            )
            ip = halves(s[4])
            s[4] = s[4] - mm(ip, halves(mm(part, ip)))
        step *= 2
    for g, (kp, qp, _, _, inv, key, query, value, b) in enumerate(state):
        ip = halves(inv)
        th_ref[g] = ip[0]
        tl_ref[g] = ip[1]
        wu = mm(ip, halves(b * jnp.concatenate([key, value], axis=1)))
        wu_ref[g] = wu
        wup = halves(wu)
        ku = mm(kp, wup, TN)
        m_hi, m_lo = halves(small_eye - ku[:, :width])
        m_ref[g, 0] = m_hi
        m_ref[g, 1] = m_lo
        off_ref[g] = ku[:, width:]
        scores = jnp.where(visible, mm(qp, kp, NT), 0.0)
        pu = mm(halves(scores), wup)
        q_hi, q_lo = halves(query - pu[:, :width])
        qe_ref[g, 0] = q_hi
        qe_ref[g, 1] = q_lo
        o0_ref[g] = pu[:, width:]


def chain_barrier(me, n):
    barrier = pltpu.get_barrier_semaphore()
    for other in (lax.rem(me + 1, n), lax.rem(me + n - 1, n)):
        pl.semaphore_signal(
            barrier, inc=1, device_id={"ctx": other}, device_id_type=pl.DeviceIdType.MESH
        )
    pl.semaphore_wait(barrier, 2)


def chain(n, place, way, heads, held, out, send_sem, recv_sem, advance):
    me = lax.axis_index("ctx")
    other = lax.rem(me + way + n, n)

    @pl.when(place == 0)
    def _():
        held[...] = jnp.zeros_like(held)

    def move(h):
        return pltpu.make_async_remote_copy(
            src_ref=out.at[h],
            dst_ref=held.at[h],
            send_sem=send_sem.at[h],
            recv_sem=recv_sem.at[h],
            device_id={"ctx": other},
            device_id_type=pl.DeviceIdType.MESH,
        )

    def step(h, carry):
        @pl.when(place > 0)
        def _():
            move(h).wait_recv()

        @pl.when(place < n - 1)
        def _():
            out[h] = advance(h, held[h]).astype(BF16)
            move(h).start()

        return carry

    lax.fori_loop(0, heads, step, 0)

    @pl.when(place < n - 1)
    def _():
        def finish(h, carry):
            move(h).wait_send()
            return carry

        lax.fori_loop(0, heads, finish, 0)


def forward_kernel(n, m_ref, off_ref, qe_ref, o0_ref, s_ref, ho_ref, held, out, send_sem, recv_sem):
    heads, width = off_ref.shape[0], off_ref.shape[1]
    me = lax.axis_index("ctx")
    chain_barrier(me, n)

    def advance(h, state):
        return mm((m_ref[h, 0], m_ref[h, 1]), (state,)) + off_ref[h]

    chain(n, me, 1, heads, held, out, send_sem, recv_sem, advance)
    s_ref[...] = held[...]
    for h in range(heads):
        ho_ref[:, h * width : (h + 1) * width] = (
            mm((qe_ref[h, 0], qe_ref[h, 1]), (held[h],)) + o0_ref[h]
        ).astype(BF16)


def backward_kernel(n, m_ref, qe_ref, do_ref, d_ref, own, held, out, send_sem, recv_sem):
    heads, width = m_ref.shape[0], m_ref.shape[2]
    me = lax.axis_index("ctx")
    chain_barrier(me, n)
    for h in range(heads):
        own[h] = mm(
            (qe_ref[h, 0], qe_ref[h, 1]), halves(do_ref[:, h * width : (h + 1) * width]), TN
        )

    def advance(h, state):
        return mm((m_ref[h, 0], m_ref[h, 1]), (state,), TN) + own[h]

    chain(n, n - 1 - me, -1, heads, held, out, send_sem, recv_sem, advance)
    d_ref[...] = held[...]


def finish_kernel(group, q_ref, k_ref, v_ref, b_ref, th_ref, tl_ref, wu_ref, s_ref, d_ref, do_ref, dq_ref, dk_ref, dv_ref, db_ref):
    length, width = q_ref.shape[0], q_ref.shape[1] // group
    rows, cols = time_ids(length, 0), time_ids(length, 1)
    visible = visible_mask(length)
    below = cols < rows
    for g in range(group):
        here = slice(g * width, (g + 1) * width)
        key = stacked(k_ref, g, width).astype(F32)
        value = stacked(v_ref, g, width).astype(F32)
        query = q_ref[:, here].astype(F32)
        k_norm, q_norm = inverse_norm(key), inverse_norm(query)
        key, query = key * k_norm, query * q_norm
        b = b_ref[g]
        kp, qp = halves(key), halves(query)
        start, end_grad = (s_ref[g],), (d_ref[g],)
        gp = halves(do_ref[:, here])
        gram = mm(kp, kp, NT)
        scores = jnp.where(visible, mm(qp, kp, NT), 0.0)
        wu = wu_ref[g]
        updates = wu[:, width:] - mm(halves(wu[:, :width]), start)
        up = halves(updates)
        update_grad = mm(halves(scores), gp, TN) + mm(kp, end_grad)
        right_grad = mm((th_ref[g], tl_ref[g]), halves(update_grad), TN)
        score_grad = halves(jnp.where(visible, mm(gp, up, NT), 0.0))
        query_grad = mm(gp, start, NT) + mm(score_grad, kp)
        system_grad = jnp.where(below, -mm(halves(right_grad), up, NT), 0.0)
        residual = value - mm(kp, start)
        db_ref[g] = jnp.sum(right_grad * residual, axis=1, keepdims=True) + jnp.sum(
            system_grad * gram, axis=1, keepdims=True
        )
        gram_grad = halves(b * system_grad)
        value_grad = b * right_grad
        key_grad = (
            mm(score_grad, qp, TN)
            + mm(up, end_grad, NT)
            - mm(halves(value_grad), start, NT)
            + mm(gram_grad, kp)
            + mm(gram_grad, kp, TN)
        )
        query_grad = q_norm * (
            query_grad - query * jnp.sum(query * query_grad, axis=1, keepdims=True)
        )
        key_grad = k_norm * (key_grad - key * jnp.sum(key * key_grad, axis=1, keepdims=True))
        dq_ref[:, here] = query_grad.astype(BF16)
        for j in range(2):
            there = slice((2 * g + j) * width, (2 * g + j + 1) * width)
            dk_ref[:, there] = key_grad[j * length : (j + 1) * length].astype(BF16)
            dv_ref[:, there] = value_grad[j * length : (j + 1) * length].astype(BF16)


def per_head(group, *shape):
    return pl.BlockSpec((group,) + shape, lambda i: (i,) + (0,) * len(shape))


def per_column(group, length, width):
    return pl.BlockSpec((length, group * width), lambda i: (0, i))


def both_halves(block):
    if lax.axis_size("tp") != 2:
        return lax.all_gather(block, "tp", axis=1, tiled=True)
    theirs = lax.ppermute(block, "tp", [(0, 1), (1, 0)])
    first = lax.axis_index("tp") == 0
    return jnp.concatenate(
        [jnp.where(first, block, theirs), jnp.where(first, theirs, block)], axis=1
    )


def mixed_share(heads_out, weight_full):
    size = lax.axis_size("tp")
    if size != 2:
        partial = jnp.dot(heads_out, weight_full.T, preferred_element_type=F32).astype(BF16)
        return lax.psum_scatter(partial, "tp", scatter_dimension=1, tiled=True)
    half = weight_full.shape[0] // 2
    me = lax.axis_index("tp")

    def part(index):
        rows = lax.dynamic_slice_in_dim(weight_full, index * half, half, 0)
        return lax.dot_general(heads_out, rows, NT, preferred_element_type=F32)

    theirs = lax.ppermute(part(1 - me).astype(BF16), "tp", [(0, 1), (1, 0)])
    return (part(me) + theirs.astype(F32)).astype(BF16)


def local(n, queries, keys, values, beta_logit, out_weight, out_grad):
    heads = beta_logit.shape[0]
    length = queries.shape[0]
    width = queries.shape[1] // heads
    double = 2 * length
    group = 2
    params = pltpu.CompilerParams(vmem_limit_bytes=LIMIT)

    weight_full = lax.all_gather(out_weight, "ctx", axis=0, tiled=True)
    grad_full = both_halves(out_grad)
    grad_cols = lax.all_to_all(grad_full, "ctx", split_axis=1, concat_axis=0, tiled=True)

    strength = 2.0 * jax.nn.sigmoid(beta_logit)
    gate = strength.reshape(heads, length, 2).transpose(0, 2, 1).reshape(heads, double, 1)

    shape = jax.ShapeDtypeStruct
    q_spec, k_spec = per_column(group, length, width), per_column(group, length, 2 * width)
    b_spec = per_head(group, double, 1)
    t_spec = per_head(group, double, double)
    wu_spec = per_head(group, double, 2 * width)
    inv_hi, inv_lo, wu, trans, offset, query_eff, own_out = pl.pallas_call(
        functools.partial(prepare_kernel, group),
        grid=(heads // group,),
        in_specs=[q_spec, k_spec, k_spec, b_spec],
        out_specs=[
            t_spec,
            t_spec,
            wu_spec,
            per_head(group, 2, width, width),
            per_head(group, width, width),
            per_head(group, 2, length, width),
            per_head(group, length, width),
        ],
        out_shape=[
            shape((heads, double, double), BF16),
            shape((heads, double, double), BF16),
            shape((heads, double, 2 * width), F32),
            shape((heads, 2, width, width), BF16),
            shape((heads, width, width), F32),
            shape((heads, 2, length, width), BF16),
            shape((heads, length, width), F32),
        ],
        compiler_params=params,
        name="prepare",
    )(queries, keys, values, gate)

    whole = pl.BlockSpec(memory_space=pltpu.VMEM)
    carried = [
        pltpu.VMEM((heads, width, width), BF16),
        pltpu.VMEM((heads, width, width), BF16),
        pltpu.SemaphoreType.DMA((heads,)),
        pltpu.SemaphoreType.DMA((heads,)),
    ]
    state_in, heads_out = pl.pallas_call(
        functools.partial(forward_kernel, n),
        in_specs=[whole] * 4,
        out_specs=[whole, whole],
        out_shape=[shape((heads, width, width), BF16), shape(queries.shape, BF16)],
        scratch_shapes=carried,
        compiler_params=pltpu.CompilerParams(
            vmem_limit_bytes=LIMIT, collective_id=0, has_side_effects=True
        ),
        name="forward_chain",
    )(trans, offset, query_eff, own_out)

    heads_full = lax.all_gather(heads_out, "ctx", axis=0, tiled=True)
    head_grad = jnp.dot(grad_full, weight_full, preferred_element_type=F32)

    state_grad = pl.pallas_call(
        functools.partial(backward_kernel, n),
        in_specs=[whole] * 3,
        out_specs=whole,
        out_shape=shape((heads, width, width), BF16),
        scratch_shapes=[pltpu.VMEM((heads, width, width), F32)] + carried,
        compiler_params=pltpu.CompilerParams(
            vmem_limit_bytes=LIMIT, collective_id=1, has_side_effects=True
        ),
        name="backward_chain",
    )(trans, query_eff, head_grad)

    heads_late, weight_late, _ = lax.optimization_barrier((heads_out, weight_full, state_grad))
    mixed = mixed_share(heads_late, weight_late)

    d_spec = per_head(group, width, width)
    query_grad, key_grad, value_grad, gate_grad = pl.pallas_call(
        functools.partial(finish_kernel, group),
        grid=(heads // group,),
        in_specs=[q_spec, k_spec, k_spec, b_spec, t_spec, t_spec, wu_spec, d_spec, d_spec, q_spec],
        out_specs=[q_spec, k_spec, k_spec, b_spec],
        out_shape=[
            shape(queries.shape, BF16),
            shape(keys.shape, BF16),
            shape(values.shape, BF16),
            shape((heads, double, 1), F32),
        ],
        compiler_params=params,
        name="finish",
    )(queries, keys, values, gate, inv_hi, inv_lo, wu, state_in, state_grad, head_grad)

    gate_grad = gate_grad.reshape(heads, 2, length).transpose(0, 2, 1).reshape(heads, double)
    logit_grad = gate_grad * strength * jax.nn.sigmoid(-beta_logit)

    heads_full, _ = lax.optimization_barrier((heads_full, query_grad))
    scale_factor = 1.0 / math.sqrt(length * n)
    weight_grad = scale_factor * lax.dot_general(
        grad_cols, heads_full, TN, preferred_element_type=F32
    )
    return (mixed, query_grad, key_grad, value_grad, logit_grad, weight_grad)


def solution(mesh):
    placed = (
        P("ctx", "tp"),
        P("ctx", "tp"),
        P("ctx", "tp"),
        P("tp", "ctx"),
        P("ctx", "tp"),
        P("ctx", "tp"),
    )
    return jax.shard_map(
        functools.partial(local, mesh.shape["ctx"]),
        mesh=mesh,
        in_specs=placed,
        out_specs=(
            P("ctx", "tp"),
            P("ctx", "tp"),
            P("ctx", "tp"),
            P("ctx", "tp"),
            P("tp", "ctx"),
            P("ctx", "tp"),
        ),
        check_vma=False,
    )
```

```python
import functools
import math

import jax
import jax.numpy as jnp
from jax import lax
from jax.experimental import pallas as pl
from jax.experimental.pallas import tpu as pltpu
from jax.sharding import PartitionSpec as P

F32 = jnp.float32
BF16 = jnp.bfloat16
NN = (((1,), (0,)), ((), ()))
NT = (((1,), (1,)), ((), ()))
TN = (((0,), (0,)), ((), ()))
LIMIT = 56 * 1024 * 1024


def halves(x):
    high = x.astype(BF16)
    return (high, (x - high.astype(F32)).astype(BF16))


def mm(left, right, dims=NN):
    total = None
    for i, a in enumerate(left):
        for j, b in enumerate(right):
            if i + j < 2:
                term = lax.dot_general(a, b, dims, preferred_element_type=F32)
                total = term if total is None else total + term
    return total


def inverse_norm(x):
    return lax.rsqrt(jnp.sum(x * x, axis=-1, keepdims=True) + 1e-06)


def stacked(ref, head, width):
    start = head * 2 * width
    return jnp.concatenate(
        [ref[:, start : start + width], ref[:, start + width : start + 2 * width]], axis=0
    )


def time_ids(length, axis):
    ids = lax.broadcasted_iota(jnp.int32, (2 * length, 2 * length), axis)
    second = (ids >= length).astype(jnp.int32)
    return 2 * (ids - second * length) + second


def visible_mask(length):
    token = lax.broadcasted_iota(jnp.int32, (length, 2 * length), 0)
    refl = lax.broadcasted_iota(jnp.int32, (length, 2 * length), 1)
    refl = jnp.where(refl >= length, refl - length, refl)
    return refl <= token


MESH = pl.DeviceIdType.MESH


class Ring:
    def __init__(self, n, block, full, sems):
        self.chips, self.block, self.full, self.sems = n // 2, block, full, sems
        self.rows = block.shape[0]
        me = lax.axis_index("ctx")
        self.me, self.core, chip = me, lax.rem(me, 2), me // 2
        self.place = jnp.where(lax.rem(chip, 2) == 0, chip // 2, self.chips - 1 - chip // 2)
        self.way = 1 - 2 * self.core
        self.partner = me + self.way
        self.next, self.prev = self.device(1, self.core), self.device(-1, self.core)

    def device(self, steps, core):
        place = lax.rem(self.place + self.way * steps + self.chips, self.chips)
        chip = jnp.where(place < self.chips // 2, 2 * place, 2 * (self.chips - 1 - place) + 1)
        return 2 * chip + core

    def copy(self, owner, sems, r, target):
        rows = pl.ds(pl.multiple_of(owner * self.rows, self.rows), self.rows)
        return pltpu.make_async_remote_copy(
            src_ref=self.full.at[rows],
            dst_ref=self.full.at[rows],
            send_sem=sems[0].at[r],
            recv_sem=sems[1].at[r],
            device_id={"ctx": target},
            device_id_type=MESH,
        )

    def along(self, r, ahead=0):
        return self.copy(self.device(-(r + ahead), self.core), self.sems[:2], r, self.next)

    def across(self, r):
        return self.copy(self.device(-r, self.core), self.sems[2:4], r, self.partner)

    def across_in(self, r):
        return self.copy(self.device(r, 1 - self.core), self.sems[2:4], r, self.partner)

    def own(self):
        rows = pl.ds(pl.multiple_of(self.me * self.rows, self.rows), self.rows)
        return pltpu.make_async_copy(self.block, self.full.at[rows], self.sems[4])

    def begin(self):
        self.own().wait()
        self.along(0).start()
        self.across(0).start()

    def pass_on(self, step, steps):
        last = self.chips - 1

        def event(r, carry):
            self.along(r, 1).wait_recv()

            @pl.when(r + 1 < last)
            def _():
                self.along(r + 1).start()

            self.across(r + 1).start()
            return carry

        low = jnp.minimum(step - 1, last)
        high = jnp.where(step == steps - 1, last, jnp.minimum(step, last))
        lax.fori_loop(low, high, event, 0)

    def end(self):
        def sent(r, carry):
            self.along(r).wait_send()
            return carry

        def both(r, carry):
            self.across(r).wait_send()
            self.across_in(r).wait_recv()
            return carry

        lax.fori_loop(0, self.chips - 1, sent, 0)
        lax.fori_loop(0, self.chips, both, 0)


def ring_scratch(n):
    dma = pltpu.SemaphoreType.DMA
    return [dma((n // 2 - 1,)), dma((n // 2 - 1,)), dma((n // 2,)), dma((n // 2,)), dma(())]


def greet(devices):
    barrier = pltpu.get_barrier_semaphore()
    for device in devices:
        pl.semaphore_signal(barrier, inc=1, device_id=device, device_id_type=MESH)
    pl.semaphore_wait(barrier, len(devices))


def columns_swap(tp, block, full, sems):
    me, cols = lax.axis_index("tp"), block.shape[1]
    sends, receives = [], []
    for d in range(1, tp):
        for kept, source in ((sends, me), (receives, lax.rem(me - d + tp, tp))):
            kept.append(
                pltpu.make_async_remote_copy(
                    src_ref=block,
                    dst_ref=full.at[:, pl.ds(pl.multiple_of(source * cols, 128), cols)],
                    send_sem=sems[0].at[d - 1],
                    recv_sem=sems[1].at[d - 1],
                    device_id={"tp": lax.rem(me + d, tp)},
                    device_id_type=MESH,
                )
            )
    own = pltpu.make_async_copy(
        block, full.at[:, pl.ds(pl.multiple_of(me * cols, 128), cols)], sems[2]
    )
    return sends, receives, own


def gather_prepare_kernel(n, tp, group, q_ref, k_ref, v_ref, b_ref, w_ref, g_ref, th_ref, tl_ref, wu_ref, m_ref, off_ref, qe_ref, o0_ref, wf_ref, gf_ref, *sems):
    step, steps = pl.program_id(0), pl.num_programs(0)
    ring = Ring(n, w_ref, wf_ref, sems[:5])
    sends, receives, own = columns_swap(tp, g_ref, gf_ref, sems[5:8])

    @pl.when(step == 0)
    def _():
        ring.own().start()
        own.start()
        peers = [{"tp": lax.rem(lax.axis_index("tp") + d, tp)} for d in range(1, tp)]
        greet([{"ctx": ring.next}, {"ctx": ring.prev}, {"ctx": ring.partner}] + peers)
        ring.begin()
        for copy in sends:
            copy.start()

    @pl.when(step > 0)
    def _():
        ring.pass_on(step, steps)

    prepare_kernel(group, q_ref, k_ref, v_ref, b_ref, th_ref, tl_ref, wu_ref, m_ref, off_ref, qe_ref, o0_ref)

    @pl.when(step == steps - 1)
    def _():
        for sent, received in zip(sends, receives):
            sent.wait_send()
            received.wait_recv()
        own.wait()
        ring.end()


def gather_finish_kernel(n, group, q_ref, k_ref, v_ref, b_ref, th_ref, tl_ref, wu_ref, s_ref, d_ref, do_ref, ho_ref, dq_ref, dk_ref, dv_ref, db_ref, hf_ref, *sems):
    step, steps = pl.program_id(0), pl.num_programs(0)
    ring = Ring(n, ho_ref, hf_ref, sems)

    @pl.when(step == 0)
    def _():
        ring.own().start()
        greet([{"ctx": ring.next}, {"ctx": ring.prev}, {"ctx": ring.partner}])
        ring.begin()

    @pl.when(step > 0)
    def _():
        ring.pass_on(step, steps)

    finish_kernel(group, q_ref, k_ref, v_ref, b_ref, th_ref, tl_ref, wu_ref, s_ref, d_ref, do_ref, dq_ref, dk_ref, dv_ref, db_ref)

    @pl.when(step == steps - 1)
    def _():
        ring.end()


def prepare_kernel(group, q_ref, k_ref, v_ref, b_ref, th_ref, tl_ref, wu_ref, m_ref, off_ref, qe_ref, o0_ref):
    length, width = q_ref.shape[0], q_ref.shape[1] // group
    rows, cols = time_ids(length, 0), time_ids(length, 1)
    visible = visible_mask(length)
    diff = rows ^ cols
    eye = (rows == cols).astype(F32)
    small_eye = (
        lax.broadcasted_iota(jnp.int32, (width, width), 0)
        == lax.broadcasted_iota(jnp.int32, (width, width), 1)
    ).astype(F32)
    state = []
    for g in range(group):
        key = stacked(k_ref, g, width).astype(F32)
        value = stacked(v_ref, g, width).astype(F32)
        query = q_ref[:, g * width : (g + 1) * width].astype(F32)
        key = key * inverse_norm(key)
        query = query * inverse_norm(query)
        b = b_ref[g]
        kp, qp = halves(key), halves(query)
        system = jnp.where(cols < rows, b * mm(kp, kp, NT), 0.0)
        ah, al = halves(system)
        inv = eye - jnp.where(diff == 1, system, 0.0)
        state.append([kp, qp, ah, al, inv, key, query, value, b])
    step = 2
    while step < 2 * length:
        inside = (diff >= step) & (diff < 2 * step)
        for s in state:
            part = (
                jnp.where(inside, s[2], jnp.zeros_like(s[2])),
                jnp.where(inside, s[3], jnp.zeros_like(s[3])),
            )
            ip = halves(s[4])
            s[4] = s[4] - mm(ip, halves(mm(part, ip)))
        step *= 2
    for g, (kp, qp, _, _, inv, key, query, value, b) in enumerate(state):
        ip = halves(inv)
        th_ref[g] = ip[0]
        tl_ref[g] = ip[1]
        wu = mm(ip, halves(b * jnp.concatenate([key, value], axis=1)))
        wu_ref[g] = wu
        wup = halves(wu)
        ku = mm(kp, wup, TN)
        m_hi, m_lo = halves(small_eye - ku[:, :width])
        m_ref[g, 0] = m_hi
        m_ref[g, 1] = m_lo
        off_ref[g] = ku[:, width:]
        scores = jnp.where(visible, mm(qp, kp, NT), 0.0)
        pu = mm(halves(scores), wup)
        q_hi, q_lo = halves(query - pu[:, :width])
        qe_ref[g, 0] = q_hi
        qe_ref[g, 1] = q_lo
        o0_ref[g] = pu[:, width:]


def chain(n, place, way, heads, held, out, send_sem, recv_sem, advance):
    me = lax.axis_index("ctx")
    other = lax.rem(me + way + n, n)

    @pl.when(place == 0)
    def _():
        held[...] = jnp.zeros_like(held)

    def move(h):
        return pltpu.make_async_remote_copy(
            src_ref=out.at[h],
            dst_ref=held.at[h],
            send_sem=send_sem.at[h],
            recv_sem=recv_sem.at[h],
            device_id={"ctx": other},
            device_id_type=pl.DeviceIdType.MESH,
        )

    def step(h, carry):
        @pl.when(place > 0)
        def _():
            move(h).wait_recv()

        @pl.when(place < n - 1)
        def _():
            out[h] = advance(h, held[h]).astype(BF16)
            move(h).start()

        return carry

    lax.fori_loop(0, heads, step, 0)

    @pl.when(place < n - 1)
    def _():
        def finish(h, carry):
            move(h).wait_send()
            return carry

        lax.fori_loop(0, heads, finish, 0)


def chains_kernel(n, m_ref, off_ref, qe_ref, o0_ref, do_ref, s_ref, d_ref, ho_ref, own, held_f, out_f, send_f, recv_f, held_b, out_b, send_b, recv_b):
    heads, width = off_ref.shape[0], off_ref.shape[1]
    me = lax.axis_index("ctx")
    greet([{"ctx": lax.rem(me + 1, n)}, {"ctx": lax.rem(me + n - 1, n)}])

    def cotangents(h, carry):
        columns = pl.ds(pl.multiple_of(h * width, width), width)
        own[h] = mm((qe_ref[h, 0], qe_ref[h, 1]), halves(do_ref[:, columns]), TN)
        return carry

    def advance(h, state):
        return mm((m_ref[h, 0], m_ref[h, 1]), (state,)) + off_ref[h]

    def retreat(h, state):
        return mm((m_ref[h, 0], m_ref[h, 1]), (state,), TN) + own[h]

    def forward():
        chain(n, me, 1, heads, held_f, out_f, send_f, recv_f, advance)

    def backward():
        chain(n, n - 1 - me, -1, heads, held_b, out_b, send_b, recv_b, retreat)

    @pl.when(me < n // 2)
    def _():
        forward()
        lax.fori_loop(0, heads, cotangents, 0)
        backward()

    @pl.when(me >= n // 2)
    def _():
        lax.fori_loop(0, heads, cotangents, 0)
        backward()
        forward()

    s_ref[...] = held_f[...]
    d_ref[...] = held_b[...]
    for h in range(heads):
        ho_ref[:, h * width : (h + 1) * width] = (
            mm((qe_ref[h, 0], qe_ref[h, 1]), (held_f[h],)) + o0_ref[h]
        ).astype(BF16)


def finish_kernel(group, q_ref, k_ref, v_ref, b_ref, th_ref, tl_ref, wu_ref, s_ref, d_ref, do_ref, dq_ref, dk_ref, dv_ref, db_ref):
    length, width = q_ref.shape[0], q_ref.shape[1] // group
    rows, cols = time_ids(length, 0), time_ids(length, 1)
    visible = visible_mask(length)
    below = cols < rows
    for g in range(group):
        here = slice(g * width, (g + 1) * width)
        key = stacked(k_ref, g, width).astype(F32)
        value = stacked(v_ref, g, width).astype(F32)
        query = q_ref[:, here].astype(F32)
        k_norm, q_norm = inverse_norm(key), inverse_norm(query)
        key, query = key * k_norm, query * q_norm
        b = b_ref[g]
        kp, qp = halves(key), halves(query)
        start, end_grad = (s_ref[g],), (d_ref[g],)
        gp = halves(do_ref[:, here])
        gram = mm(kp, kp, NT)
        scores = jnp.where(visible, mm(qp, kp, NT), 0.0)
        wu = wu_ref[g]
        updates = wu[:, width:] - mm(halves(wu[:, :width]), start)
        up = halves(updates)
        update_grad = mm(halves(scores), gp, TN) + mm(kp, end_grad)
        right_grad = mm((th_ref[g], tl_ref[g]), halves(update_grad), TN)
        score_grad = halves(jnp.where(visible, mm(gp, up, NT), 0.0))
        query_grad = mm(gp, start, NT) + mm(score_grad, kp)
        system_grad = jnp.where(below, -mm(halves(right_grad), up, NT), 0.0)
        residual = value - mm(kp, start)
        db_ref[g] = jnp.sum(right_grad * residual, axis=1, keepdims=True) + jnp.sum(
            system_grad * gram, axis=1, keepdims=True
        )
        gram_grad = halves(b * system_grad)
        value_grad = b * right_grad
        key_grad = (
            mm(score_grad, qp, TN)
            + mm(up, end_grad, NT)
            - mm(halves(value_grad), start, NT)
            + mm(gram_grad, kp)
            + mm(gram_grad, kp, TN)
        )
        query_grad = q_norm * (
            query_grad - query * jnp.sum(query * query_grad, axis=1, keepdims=True)
        )
        key_grad = k_norm * (key_grad - key * jnp.sum(key * key_grad, axis=1, keepdims=True))
        dq_ref[:, here] = query_grad.astype(BF16)
        for j in range(2):
            there = slice((2 * g + j) * width, (2 * g + j + 1) * width)
            dk_ref[:, there] = key_grad[j * length : (j + 1) * length].astype(BF16)
            dv_ref[:, there] = value_grad[j * length : (j + 1) * length].astype(BF16)


def per_head(group, *shape):
    return pl.BlockSpec((group,) + shape, lambda i: (i,) + (0,) * len(shape))


def per_column(group, length, width):
    return pl.BlockSpec((length, group * width), lambda i: (0, i))


def mixed_share(heads_out, weight_full):
    size = lax.axis_size("tp")
    if size != 2:
        partial = jnp.dot(heads_out, weight_full.T, preferred_element_type=F32).astype(BF16)
        return lax.psum_scatter(partial, "tp", scatter_dimension=1, tiled=True)
    half = weight_full.shape[0] // 2
    me = lax.axis_index("tp")

    def part(index):
        rows = lax.dynamic_slice_in_dim(weight_full, index * half, half, 0)
        return lax.dot_general(heads_out, rows, NT, preferred_element_type=F32)

    theirs = lax.ppermute(part(1 - me).astype(BF16), "tp", [(0, 1), (1, 0)])
    return (part(me) + theirs.astype(F32)).astype(BF16)


def local(n, queries, keys, values, beta_logit, out_weight, out_grad):
    heads = beta_logit.shape[0]
    length = queries.shape[0]
    width = queries.shape[1] // heads
    double = 2 * length
    group = 2
    tp = lax.axis_size("tp")
    model = out_weight.shape[0] * n
    anywhere = pl.BlockSpec(memory_space=pl.ANY)
    dma = pltpu.SemaphoreType.DMA

    def params(number):
        return pltpu.CompilerParams(
            vmem_limit_bytes=LIMIT, collective_id=number, has_side_effects=True
        )

    strength = 2.0 * jax.nn.sigmoid(beta_logit)
    gate = strength.reshape(heads, length, 2).transpose(0, 2, 1).reshape(heads, double, 1)

    shape = jax.ShapeDtypeStruct
    q_spec, k_spec = per_column(group, length, width), per_column(group, length, 2 * width)
    b_spec = per_head(group, double, 1)
    t_spec = per_head(group, double, double)
    wu_spec = per_head(group, double, 2 * width)
    inv_hi, inv_lo, wu, trans, offset, query_eff, own_out, weight_full, grad_full = pl.pallas_call(
        functools.partial(gather_prepare_kernel, n, tp, group),
        grid=(heads // group,),
        in_specs=[q_spec, k_spec, k_spec, b_spec, anywhere, anywhere],
        out_specs=[
            t_spec,
            t_spec,
            wu_spec,
            per_head(group, 2, width, width),
            per_head(group, width, width),
            per_head(group, 2, length, width),
            per_head(group, length, width),
            anywhere,
            anywhere,
        ],
        out_shape=[
            shape((heads, double, double), BF16),
            shape((heads, double, double), BF16),
            shape((heads, double, 2 * width), F32),
            shape((heads, 2, width, width), BF16),
            shape((heads, width, width), F32),
            shape((heads, 2, length, width), BF16),
            shape((heads, length, width), F32),
            shape((model, out_weight.shape[1]), BF16),
            shape((length, model), BF16),
        ],
        scratch_shapes=ring_scratch(n) + [dma((max(tp - 1, 1),)), dma((max(tp - 1, 1),)), dma(())],
        compiler_params=params(0),
        name="prepare",
    )(queries, keys, values, gate, out_weight, out_grad)
    grad_cols = lax.all_to_all(grad_full, "ctx", split_axis=1, concat_axis=0, tiled=True)
    head_grad = jnp.dot(grad_full, weight_full, preferred_element_type=F32)
    head_grad, grad_cols = lax.optimization_barrier((head_grad, grad_cols))

    whole = pl.BlockSpec(memory_space=pltpu.VMEM)
    carried = [
        pltpu.VMEM((heads, width, width), BF16),
        pltpu.VMEM((heads, width, width), BF16),
        pltpu.SemaphoreType.DMA((heads,)),
        pltpu.SemaphoreType.DMA((heads,)),
    ]
    state_in, state_grad, heads_out = pl.pallas_call(
        functools.partial(chains_kernel, n),
        in_specs=[whole] * 5,
        out_specs=[whole] * 3,
        out_shape=[
            shape((heads, width, width), BF16),
            shape((heads, width, width), BF16),
            shape(queries.shape, BF16),
        ],
        scratch_shapes=[pltpu.VMEM((heads, width, width), F32)] + carried + carried,
        compiler_params=params(1),
        name="chains",
    )(trans, offset, query_eff, own_out, head_grad)
    mixed = mixed_share(heads_out, weight_full)

    d_spec = per_head(group, width, width)
    query_grad, key_grad, value_grad, gate_grad, heads_full = pl.pallas_call(
        functools.partial(gather_finish_kernel, n, group),
        grid=(heads // group,),
        in_specs=[q_spec, k_spec, k_spec, b_spec, t_spec, t_spec, wu_spec, d_spec, d_spec, q_spec, anywhere],
        out_specs=[q_spec, k_spec, k_spec, b_spec, anywhere],
        out_shape=[
            shape(queries.shape, BF16),
            shape(keys.shape, BF16),
            shape(values.shape, BF16),
            shape((heads, double, 1), F32),
            shape((length * n, queries.shape[1]), BF16),
        ],
        scratch_shapes=ring_scratch(n),
        compiler_params=params(2),
        name="finish",
    )(queries, keys, values, gate, inv_hi, inv_lo, wu, state_in, state_grad, head_grad, heads_out)

    gate_grad = gate_grad.reshape(heads, 2, length).transpose(0, 2, 1).reshape(heads, double)
    logit_grad = gate_grad * strength * jax.nn.sigmoid(-beta_logit)

    scale_factor = 1.0 / math.sqrt(length * n)
    weight_grad = scale_factor * lax.dot_general(
        grad_cols, heads_full, TN, preferred_element_type=F32
    )
    return (mixed, query_grad, key_grad, value_grad, logit_grad, weight_grad)


def solution(mesh):
    placed = (
        P("ctx", "tp"),
        P("ctx", "tp"),
        P("ctx", "tp"),
        P("tp", "ctx"),
        P("ctx", "tp"),
        P("ctx", "tp"),
    )
    return jax.shard_map(
        functools.partial(local, mesh.shape["ctx"]),
        mesh=mesh,
        in_specs=placed,
        out_specs=(
            P("ctx", "tp"),
            P("ctx", "tp"),
            P("ctx", "tp"),
            P("ctx", "tp"),
            P("tp", "ctx"),
            P("ctx", "tp"),
        ),
        check_vma=False,
    )
```

```python
import functools
import math

import jax
import jax.numpy as jnp
from jax import lax
from jax.experimental import pallas as pl
from jax.experimental.pallas import tpu as pltpu
from jax.sharding import PartitionSpec as P

F32 = jnp.float32
BF16 = jnp.bfloat16
NN = (((1,), (0,)), ((), ()))
NT = (((1,), (1,)), ((), ()))
TN = (((0,), (0,)), ((), ()))
LIMIT = 56 * 1024 * 1024


def halves(x):
    high = x.astype(BF16)
    return (high, (x - high.astype(F32)).astype(BF16))


def mm(left, right, dims=NN):
    total = None
    for i, a in enumerate(left):
        for j, b in enumerate(right):
            if i + j < 2:
                term = lax.dot_general(a, b, dims, preferred_element_type=F32)
                total = term if total is None else total + term
    return total


def inverse_norm(x):
    return lax.rsqrt(jnp.sum(x * x, axis=-1, keepdims=True) + 1e-06)


def stacked(ref, head, width):
    start = head * 2 * width
    return jnp.concatenate(
        [ref[:, start : start + width], ref[:, start + width : start + 2 * width]], axis=0
    )


def time_ids(length, axis):
    ids = lax.broadcasted_iota(jnp.int32, (2 * length, 2 * length), axis)
    second = (ids >= length).astype(jnp.int32)
    return 2 * (ids - second * length) + second


def visible_mask(length):
    token = lax.broadcasted_iota(jnp.int32, (length, 2 * length), 0)
    refl = lax.broadcasted_iota(jnp.int32, (length, 2 * length), 1)
    refl = jnp.where(refl >= length, refl - length, refl)
    return refl <= token


MESH = pl.DeviceIdType.MESH
PARTS = 4


class Ring:
    def __init__(self, n, block, full, sems):
        self.chips, self.block, self.full, self.sems = n // 2, block, full, sems
        self.rows = block.shape[0]
        me = lax.axis_index("ctx")
        self.me, self.core, chip = me, lax.rem(me, 2), me // 2
        self.place = jnp.where(lax.rem(chip, 2) == 0, chip // 2, self.chips - 1 - chip // 2)
        self.way = 1 - 2 * self.core
        self.partner = me + self.way
        self.next, self.prev = self.device(1, self.core), self.device(-1, self.core)

    def device(self, steps, core):
        place = lax.rem(self.place + self.way * steps + self.chips, self.chips)
        chip = jnp.where(place < self.chips // 2, 2 * place, 2 * (self.chips - 1 - place) + 1)
        return 2 * chip + core

    def copy(self, owner, sems, r, part, target):
        size = self.rows // PARTS
        rows = pl.ds(pl.multiple_of(owner * self.rows + part * size, size), size)
        return pltpu.make_async_remote_copy(
            src_ref=self.full.at[rows],
            dst_ref=self.full.at[rows],
            send_sem=sems[0].at[r, part],
            recv_sem=sems[1].at[r, part],
            device_id={"ctx": target},
            device_id_type=MESH,
        )

    def along(self, r, part, ahead=0):
        return self.copy(self.device(-(r + ahead), self.core), self.sems[:2], r, part, self.next)

    def across(self, r, part):
        return self.copy(self.device(-r, self.core), self.sems[2:4], r, part, self.partner)

    def across_in(self, r, part):
        return self.copy(self.device(r, 1 - self.core), self.sems[2:4], r, part, self.partner)

    def own(self):
        rows = pl.ds(pl.multiple_of(self.me * self.rows, self.rows), self.rows)
        return pltpu.make_async_copy(self.block, self.full.at[rows], self.sems[4])

    def begin(self):
        self.own().wait()
        for part in range(PARTS):
            self.along(0, part).start()
        for part in range(PARTS):
            self.across(0, part).start()

    def pass_on(self, step, steps):
        last = self.chips - 1

        def event(r, carry):
            for part in range(PARTS):
                self.along(r, part, 1).wait_recv()

                @pl.when(r + 1 < last)
                def _():
                    self.along(r + 1, part).start()

                self.across(r + 1, part).start()
            return carry

        low = jnp.minimum(step - 1, last)
        high = jnp.where(step == steps - 1, last, jnp.minimum(step, last))
        lax.fori_loop(low, high, event, 0)

    def end(self):
        def sent(r, carry):
            for part in range(PARTS):
                self.along(r, part).wait_send()
            return carry

        def both(r, carry):
            for part in range(PARTS):
                self.across(r, part).wait_send()
                self.across_in(r, part).wait_recv()
            return carry

        lax.fori_loop(0, self.chips - 1, sent, 0)
        lax.fori_loop(0, self.chips, both, 0)


def ring_scratch(n):
    dma = pltpu.SemaphoreType.DMA
    steps, blocks = (n // 2 - 1, PARTS), (n // 2, PARTS)
    return [dma(steps), dma(steps), dma(blocks), dma(blocks), dma(())]


def greet(devices):
    barrier = pltpu.get_barrier_semaphore()
    for device in devices:
        pl.semaphore_signal(barrier, inc=1, device_id=device, device_id_type=MESH)
    pl.semaphore_wait(barrier, len(devices))


def columns_swap(tp, block, full, sems):
    me, cols = lax.axis_index("tp"), block.shape[1]
    sends, receives = [], []
    for d in range(1, tp):
        for kept, source in ((sends, me), (receives, lax.rem(me - d + tp, tp))):
            kept.append(
                pltpu.make_async_remote_copy(
                    src_ref=block,
                    dst_ref=full.at[:, pl.ds(pl.multiple_of(source * cols, 128), cols)],
                    send_sem=sems[0].at[d - 1],
                    recv_sem=sems[1].at[d - 1],
                    device_id={"tp": lax.rem(me + d, tp)},
                    device_id_type=MESH,
                )
            )
    own = pltpu.make_async_copy(
        block, full.at[:, pl.ds(pl.multiple_of(me * cols, 128), cols)], sems[2]
    )
    return sends, receives, own


def gather_prepare_kernel(n, tp, group, q_ref, k_ref, v_ref, b_ref, w_ref, g_ref, th_ref, tl_ref, wu_ref, m_ref, off_ref, qe_ref, o0_ref, wf_ref, gf_ref, *sems):
    step, steps = pl.program_id(0), pl.num_programs(0)
    ring = Ring(n, w_ref, wf_ref, sems[:5])
    sends, receives, own = columns_swap(tp, g_ref, gf_ref, sems[5:8])

    @pl.when(step == 0)
    def _():
        ring.own().start()
        own.start()
        peers = [{"tp": lax.rem(lax.axis_index("tp") + d, tp)} for d in range(1, tp)]
        greet([{"ctx": ring.next}, {"ctx": ring.prev}, {"ctx": ring.partner}] + peers)
        ring.begin()
        for copy in sends:
            copy.start()

    @pl.when(step > 0)
    def _():
        ring.pass_on(step, steps)

    prepare_kernel(group, q_ref, k_ref, v_ref, b_ref, th_ref, tl_ref, wu_ref, m_ref, off_ref, qe_ref, o0_ref)

    @pl.when(step == steps - 1)
    def _():
        for sent, received in zip(sends, receives):
            sent.wait_send()
            received.wait_recv()
        own.wait()
        ring.end()


def gather_finish_kernel(n, group, q_ref, k_ref, v_ref, b_ref, th_ref, tl_ref, wu_ref, s_ref, d_ref, do_ref, ho_ref, dq_ref, dk_ref, dv_ref, db_ref, hf_ref, *sems):
    step, steps = pl.program_id(0), pl.num_programs(0)
    ring = Ring(n, ho_ref, hf_ref, sems)

    @pl.when(step == 0)
    def _():
        ring.own().start()
        greet([{"ctx": ring.next}, {"ctx": ring.prev}, {"ctx": ring.partner}])
        ring.begin()

    @pl.when(step > 0)
    def _():
        ring.pass_on(step, steps)

    finish_kernel(group, q_ref, k_ref, v_ref, b_ref, th_ref, tl_ref, wu_ref, s_ref, d_ref, do_ref, dq_ref, dk_ref, dv_ref, db_ref)

    @pl.when(step == steps - 1)
    def _():
        ring.end()


def prepare_kernel(group, q_ref, k_ref, v_ref, b_ref, th_ref, tl_ref, wu_ref, m_ref, off_ref, qe_ref, o0_ref):
    length, width = q_ref.shape[0], q_ref.shape[1] // group
    rows, cols = time_ids(length, 0), time_ids(length, 1)
    visible = visible_mask(length)
    diff = rows ^ cols
    eye = (rows == cols).astype(F32)
    small_eye = (
        lax.broadcasted_iota(jnp.int32, (width, width), 0)
        == lax.broadcasted_iota(jnp.int32, (width, width), 1)
    ).astype(F32)
    state = []
    for g in range(group):
        key = stacked(k_ref, g, width).astype(F32)
        value = stacked(v_ref, g, width).astype(F32)
        query = q_ref[:, g * width : (g + 1) * width].astype(F32)
        key = key * inverse_norm(key)
        query = query * inverse_norm(query)
        b = b_ref[g]
        kp, qp = halves(key), halves(query)
        system = jnp.where(cols < rows, b * mm(kp, kp, NT), 0.0)
        ah, al = halves(system)
        inv = eye - jnp.where(diff == 1, system, 0.0)
        state.append([kp, qp, ah, al, inv, key, query, value, b])
    step = 2
    while step < 2 * length:
        inside = (diff >= step) & (diff < 2 * step)
        for s in state:
            part = (
                jnp.where(inside, s[2], jnp.zeros_like(s[2])),
                jnp.where(inside, s[3], jnp.zeros_like(s[3])),
            )
            ip = halves(s[4])
            s[4] = s[4] - mm(ip, halves(mm(part, ip)))
        step *= 2
    for g, (kp, qp, _, _, inv, key, query, value, b) in enumerate(state):
        ip = halves(inv)
        th_ref[g] = ip[0]
        tl_ref[g] = ip[1]
        wu = mm(ip, halves(b * jnp.concatenate([key, value], axis=1)))
        wu_ref[g] = wu
        wup = halves(wu)
        ku = mm(kp, wup, TN)
        m_hi, m_lo = halves(small_eye - ku[:, :width])
        m_ref[g, 0] = m_hi
        m_ref[g, 1] = m_lo
        off_ref[g] = ku[:, width:]
        scores = jnp.where(visible, mm(qp, kp, NT), 0.0)
        pu = mm(halves(scores), wup)
        q_hi, q_lo = halves(query - pu[:, :width])
        qe_ref[g, 0] = q_hi
        qe_ref[g, 1] = q_lo
        o0_ref[g] = pu[:, width:]


def chain(n, place, way, heads, held, out, send_sem, recv_sem, advance):
    me = lax.axis_index("ctx")
    other = lax.rem(me + way + n, n)

    @pl.when(place == 0)
    def _():
        held[...] = jnp.zeros_like(held)

    def move(h):
        return pltpu.make_async_remote_copy(
            src_ref=out.at[h],
            dst_ref=held.at[h],
            send_sem=send_sem.at[h],
            recv_sem=recv_sem.at[h],
            device_id={"ctx": other},
            device_id_type=pl.DeviceIdType.MESH,
        )

    def step(h, carry):
        @pl.when(place > 0)
        def _():
            move(h).wait_recv()

        @pl.when(place < n - 1)
        def _():
            out[h] = advance(h, held[h]).astype(BF16)
            move(h).start()

        return carry

    lax.fori_loop(0, heads, step, 0)

    @pl.when(place < n - 1)
    def _():
        def finish(h, carry):
            move(h).wait_send()
            return carry

        lax.fori_loop(0, heads, finish, 0)


def chains_kernel(n, m_ref, off_ref, qe_ref, o0_ref, do_ref, s_ref, d_ref, ho_ref, own, held_f, out_f, send_f, recv_f, held_b, out_b, send_b, recv_b):
    heads, width = off_ref.shape[0], off_ref.shape[1]
    me = lax.axis_index("ctx")
    greet([{"ctx": lax.rem(me + 1, n)}, {"ctx": lax.rem(me + n - 1, n)}])

    def cotangents(h, carry):
        columns = pl.ds(pl.multiple_of(h * width, width), width)
        own[h] = mm((qe_ref[h, 0], qe_ref[h, 1]), halves(do_ref[:, columns]), TN)
        return carry

    def advance(h, state):
        return mm((m_ref[h, 0], m_ref[h, 1]), (state,)) + off_ref[h]

    def retreat(h, state):
        return mm((m_ref[h, 0], m_ref[h, 1]), (state,), TN) + own[h]

    def forward():
        chain(n, me, 1, heads, held_f, out_f, send_f, recv_f, advance)

    def backward():
        chain(n, n - 1 - me, -1, heads, held_b, out_b, send_b, recv_b, retreat)

    @pl.when(me < n // 2)
    def _():
        forward()
        lax.fori_loop(0, heads, cotangents, 0)
        backward()

    @pl.when(me >= n // 2)
    def _():
        lax.fori_loop(0, heads, cotangents, 0)
        backward()
        forward()

    s_ref[...] = held_f[...]
    d_ref[...] = held_b[...]
    for h in range(heads):
        ho_ref[:, h * width : (h + 1) * width] = (
            mm((qe_ref[h, 0], qe_ref[h, 1]), (held_f[h],)) + o0_ref[h]
        ).astype(BF16)


def finish_kernel(group, q_ref, k_ref, v_ref, b_ref, th_ref, tl_ref, wu_ref, s_ref, d_ref, do_ref, dq_ref, dk_ref, dv_ref, db_ref):
    length, width = q_ref.shape[0], q_ref.shape[1] // group
    rows, cols = time_ids(length, 0), time_ids(length, 1)
    visible = visible_mask(length)
    below = cols < rows
    for g in range(group):
        here = slice(g * width, (g + 1) * width)
        key = stacked(k_ref, g, width).astype(F32)
        value = stacked(v_ref, g, width).astype(F32)
        query = q_ref[:, here].astype(F32)
        k_norm, q_norm = inverse_norm(key), inverse_norm(query)
        key, query = key * k_norm, query * q_norm
        b = b_ref[g]
        kp, qp = halves(key), halves(query)
        start, end_grad = (s_ref[g],), (d_ref[g],)
        gp = halves(do_ref[:, here])
        gram = mm(kp, kp, NT)
        scores = jnp.where(visible, mm(qp, kp, NT), 0.0)
        wu = wu_ref[g]
        updates = wu[:, width:] - mm(halves(wu[:, :width]), start)
        up = halves(updates)
        update_grad = mm(halves(scores), gp, TN) + mm(kp, end_grad)
        right_grad = mm((th_ref[g], tl_ref[g]), halves(update_grad), TN)
        score_grad = halves(jnp.where(visible, mm(gp, up, NT), 0.0))
        query_grad = mm(gp, start, NT) + mm(score_grad, kp)
        system_grad = jnp.where(below, -mm(halves(right_grad), up, NT), 0.0)
        residual = value - mm(kp, start)
        db_ref[g] = jnp.sum(right_grad * residual, axis=1, keepdims=True) + jnp.sum(
            system_grad * gram, axis=1, keepdims=True
        )
        gram_grad = halves(b * system_grad)
        value_grad = b * right_grad
        key_grad = (
            mm(score_grad, qp, TN)
            + mm(up, end_grad, NT)
            - mm(halves(value_grad), start, NT)
            + mm(gram_grad, kp)
            + mm(gram_grad, kp, TN)
        )
        query_grad = q_norm * (
            query_grad - query * jnp.sum(query * query_grad, axis=1, keepdims=True)
        )
        key_grad = k_norm * (key_grad - key * jnp.sum(key * key_grad, axis=1, keepdims=True))
        dq_ref[:, here] = query_grad.astype(BF16)
        for j in range(2):
            there = slice((2 * g + j) * width, (2 * g + j + 1) * width)
            dk_ref[:, there] = key_grad[j * length : (j + 1) * length].astype(BF16)
            dv_ref[:, there] = value_grad[j * length : (j + 1) * length].astype(BF16)


def per_head(group, *shape):
    return pl.BlockSpec((group,) + shape, lambda i: (i,) + (0,) * len(shape))


def per_column(group, length, width):
    return pl.BlockSpec((length, group * width), lambda i: (0, i))


def mixed_share(heads_out, weight_full):
    size = lax.axis_size("tp")
    if size != 2:
        partial = jnp.dot(heads_out, weight_full.T, preferred_element_type=F32).astype(BF16)
        return lax.psum_scatter(partial, "tp", scatter_dimension=1, tiled=True)
    half = weight_full.shape[0] // 2
    me = lax.axis_index("tp")

    def part(index):
        rows = lax.dynamic_slice_in_dim(weight_full, index * half, half, 0)
        return lax.dot_general(heads_out, rows, NT, preferred_element_type=F32)

    theirs = lax.ppermute(part(1 - me).astype(BF16), "tp", [(0, 1), (1, 0)])
    return (part(me) + theirs.astype(F32)).astype(BF16)


def local(n, queries, keys, values, beta_logit, out_weight, out_grad):
    heads = beta_logit.shape[0]
    length = queries.shape[0]
    width = queries.shape[1] // heads
    double = 2 * length
    group = 2
    tp = lax.axis_size("tp")
    model = out_weight.shape[0] * n
    anywhere = pl.BlockSpec(memory_space=pl.ANY)
    dma = pltpu.SemaphoreType.DMA

    def params(number):
        return pltpu.CompilerParams(
            vmem_limit_bytes=LIMIT, collective_id=number, has_side_effects=True
        )

    strength = 2.0 * jax.nn.sigmoid(beta_logit)
    gate = strength.reshape(heads, length, 2).transpose(0, 2, 1).reshape(heads, double, 1)

    shape = jax.ShapeDtypeStruct
    q_spec, k_spec = per_column(group, length, width), per_column(group, length, 2 * width)
    b_spec = per_head(group, double, 1)
    t_spec = per_head(group, double, double)
    wu_spec = per_head(group, double, 2 * width)
    inv_hi, inv_lo, wu, trans, offset, query_eff, own_out, weight_full, grad_full = pl.pallas_call(
        functools.partial(gather_prepare_kernel, n, tp, group),
        grid=(heads // group,),
        in_specs=[q_spec, k_spec, k_spec, b_spec, anywhere, anywhere],
        out_specs=[
            t_spec,
            t_spec,
            wu_spec,
            per_head(group, 2, width, width),
            per_head(group, width, width),
            per_head(group, 2, length, width),
            per_head(group, length, width),
            anywhere,
            anywhere,
        ],
        out_shape=[
            shape((heads, double, double), BF16),
            shape((heads, double, double), BF16),
            shape((heads, double, 2 * width), F32),
            shape((heads, 2, width, width), BF16),
            shape((heads, width, width), F32),
            shape((heads, 2, length, width), BF16),
            shape((heads, length, width), F32),
            shape((model, out_weight.shape[1]), BF16),
            shape((length, model), BF16),
        ],
        scratch_shapes=ring_scratch(n) + [dma((max(tp - 1, 1),)), dma((max(tp - 1, 1),)), dma(())],
        compiler_params=params(0),
        name="prepare",
    )(queries, keys, values, gate, out_weight, out_grad)
    grad_cols = lax.all_to_all(grad_full, "ctx", split_axis=1, concat_axis=0, tiled=True)
    head_grad = jnp.dot(grad_full, weight_full, preferred_element_type=F32)
    head_grad, grad_cols = lax.optimization_barrier((head_grad, grad_cols))

    whole = pl.BlockSpec(memory_space=pltpu.VMEM)
    carried = [
        pltpu.VMEM((heads, width, width), BF16),
        pltpu.VMEM((heads, width, width), BF16),
        pltpu.SemaphoreType.DMA((heads,)),
        pltpu.SemaphoreType.DMA((heads,)),
    ]
    state_in, state_grad, heads_out = pl.pallas_call(
        functools.partial(chains_kernel, n),
        in_specs=[whole] * 5,
        out_specs=[whole] * 3,
        out_shape=[
            shape((heads, width, width), BF16),
            shape((heads, width, width), BF16),
            shape(queries.shape, BF16),
        ],
        scratch_shapes=[pltpu.VMEM((heads, width, width), F32)] + carried + carried,
        compiler_params=params(1),
        name="chains",
    )(trans, offset, query_eff, own_out, head_grad)
    mixed = mixed_share(heads_out, weight_full)

    d_spec = per_head(group, width, width)
    query_grad, key_grad, value_grad, gate_grad, heads_full = pl.pallas_call(
        functools.partial(gather_finish_kernel, n, group),
        grid=(heads // group,),
        in_specs=[q_spec, k_spec, k_spec, b_spec, t_spec, t_spec, wu_spec, d_spec, d_spec, q_spec, anywhere],
        out_specs=[q_spec, k_spec, k_spec, b_spec, anywhere],
        out_shape=[
            shape(queries.shape, BF16),
            shape(keys.shape, BF16),
            shape(values.shape, BF16),
            shape((heads, double, 1), F32),
            shape((length * n, queries.shape[1]), BF16),
        ],
        scratch_shapes=ring_scratch(n),
        compiler_params=params(2),
        name="finish",
    )(queries, keys, values, gate, inv_hi, inv_lo, wu, state_in, state_grad, head_grad, heads_out)

    gate_grad = gate_grad.reshape(heads, 2, length).transpose(0, 2, 1).reshape(heads, double)
    logit_grad = gate_grad * strength * jax.nn.sigmoid(-beta_logit)

    scale_factor = 1.0 / math.sqrt(length * n)
    weight_grad = scale_factor * lax.dot_general(
        grad_cols, heads_full, TN, preferred_element_type=F32
    )
    return (mixed, query_grad, key_grad, value_grad, logit_grad, weight_grad)


def solution(mesh):
    placed = (
        P("ctx", "tp"),
        P("ctx", "tp"),
        P("ctx", "tp"),
        P("tp", "ctx"),
        P("ctx", "tp"),
        P("ctx", "tp"),
    )
    return jax.shard_map(
        functools.partial(local, mesh.shape["ctx"]),
        mesh=mesh,
        in_specs=placed,
        out_specs=(
            P("ctx", "tp"),
            P("ctx", "tp"),
            P("ctx", "tp"),
            P("ctx", "tp"),
            P("tp", "ctx"),
            P("ctx", "tp"),
        ),
        check_vma=False,
    )
```

```python
import functools
import math

import jax
import jax.numpy as jnp
from jax import lax
from jax.experimental import pallas as pl
from jax.experimental.pallas import tpu as pltpu
from jax.sharding import PartitionSpec as P

F32 = jnp.float32
BF16 = jnp.bfloat16
NN = (((1,), (0,)), ((), ()))
NT = (((1,), (1,)), ((), ()))
TN = (((0,), (0,)), ((), ()))
LIMIT = 56 * 1024 * 1024


def halves(x):
    high = x.astype(BF16)
    return (high, (x - high.astype(F32)).astype(BF16))


def mm(left, right, dims=NN):
    total = None
    for i, a in enumerate(left):
        for j, b in enumerate(right):
            if i + j < 2:
                term = lax.dot_general(a, b, dims, preferred_element_type=F32)
                total = term if total is None else total + term
    return total


def inverse_norm(x):
    return lax.rsqrt(jnp.sum(x * x, axis=-1, keepdims=True) + 1e-06)


def stacked(ref, head, width):
    start = head * 2 * width
    return jnp.concatenate(
        [ref[:, start : start + width], ref[:, start + width : start + 2 * width]], axis=0
    )


def time_ids(length, axis):
    ids = lax.broadcasted_iota(jnp.int32, (2 * length, 2 * length), axis)
    second = (ids >= length).astype(jnp.int32)
    return 2 * (ids - second * length) + second


def visible_mask(length):
    token = lax.broadcasted_iota(jnp.int32, (length, 2 * length), 0)
    refl = lax.broadcasted_iota(jnp.int32, (length, 2 * length), 1)
    refl = jnp.where(refl >= length, refl - length, refl)
    return refl <= token


MESH = pl.DeviceIdType.MESH


def greet(devices):
    barrier = pltpu.get_barrier_semaphore()
    for device in devices:
        pl.semaphore_signal(barrier, inc=1, device_id=device, device_id_type=MESH)
    pl.semaphore_wait(barrier, len(devices))


def columns_swap(tp, block, full, sems):
    me, cols = lax.axis_index("tp"), block.shape[1]
    sends, receives = [], []
    for d in range(1, tp):
        for kept, source in ((sends, me), (receives, lax.rem(me - d + tp, tp))):
            kept.append(
                pltpu.make_async_remote_copy(
                    src_ref=block,
                    dst_ref=full.at[:, pl.ds(pl.multiple_of(source * cols, 128), cols)],
                    send_sem=sems[0].at[d - 1],
                    recv_sem=sems[1].at[d - 1],
                    device_id={"tp": lax.rem(me + d, tp)},
                    device_id_type=MESH,
                )
            )
    own = pltpu.make_async_copy(
        block, full.at[:, pl.ds(pl.multiple_of(me * cols, 128), cols)], sems[2]
    )
    return sends, receives, own


def swap_prepare_kernel(tp, group, q_ref, k_ref, v_ref, b_ref, g_ref, th_ref, tl_ref, wu_ref, m_ref, off_ref, qe_ref, o0_ref, gf_ref, *sems):
    step, steps = pl.program_id(0), pl.num_programs(0)
    sends, receives, own = columns_swap(tp, g_ref, gf_ref, sems)

    @pl.when(step == 0)
    def _():
        own.start()
        greet([{"tp": lax.rem(lax.axis_index("tp") + d, tp)} for d in range(1, tp)])
        for copy in sends:
            copy.start()

    prepare_kernel(group, q_ref, k_ref, v_ref, b_ref, th_ref, tl_ref, wu_ref, m_ref, off_ref, qe_ref, o0_ref)

    @pl.when(step == steps - 1)
    def _():
        for sent, received in zip(sends, receives):
            sent.wait_send()
            received.wait_recv()
        own.wait()


def prepare_kernel(group, q_ref, k_ref, v_ref, b_ref, th_ref, tl_ref, wu_ref, m_ref, off_ref, qe_ref, o0_ref):
    length, width = q_ref.shape[0], q_ref.shape[1] // group
    rows, cols = time_ids(length, 0), time_ids(length, 1)
    visible = visible_mask(length)
    diff = rows ^ cols
    eye = (rows == cols).astype(F32)
    small_eye = (
        lax.broadcasted_iota(jnp.int32, (width, width), 0)
        == lax.broadcasted_iota(jnp.int32, (width, width), 1)
    ).astype(F32)
    state = []
    for g in range(group):
        key = stacked(k_ref, g, width).astype(F32)
        value = stacked(v_ref, g, width).astype(F32)
        query = q_ref[:, g * width : (g + 1) * width].astype(F32)
        key = key * inverse_norm(key)
        query = query * inverse_norm(query)
        b = b_ref[g]
        kp, qp = halves(key), halves(query)
        system = jnp.where(cols < rows, b * mm(kp, kp, NT), 0.0)
        ah, al = halves(system)
        inv = eye - jnp.where(diff == 1, system, 0.0)
        state.append([kp, qp, ah, al, inv, key, query, value, b])
    step = 2
    while step < 2 * length:
        inside = (diff >= step) & (diff < 2 * step)
        for s in state:
            part = (
                jnp.where(inside, s[2], jnp.zeros_like(s[2])),
                jnp.where(inside, s[3], jnp.zeros_like(s[3])),
            )
            ip = halves(s[4])
            s[4] = s[4] - mm(ip, halves(mm(part, ip)))
        step *= 2
    for g, (kp, qp, _, _, inv, key, query, value, b) in enumerate(state):
        ip = halves(inv)
        th_ref[g] = ip[0]
        tl_ref[g] = ip[1]
        wu = mm(ip, halves(b * jnp.concatenate([key, value], axis=1)))
        wu_ref[g] = wu
        wup = halves(wu)
        ku = mm(kp, wup, TN)
        m_hi, m_lo = halves(small_eye - ku[:, :width])
        m_ref[g, 0] = m_hi
        m_ref[g, 1] = m_lo
        off_ref[g] = ku[:, width:]
        scores = jnp.where(visible, mm(qp, kp, NT), 0.0)
        pu = mm(halves(scores), wup)
        q_hi, q_lo = halves(query - pu[:, :width])
        qe_ref[g, 0] = q_hi
        qe_ref[g, 1] = q_lo
        o0_ref[g] = pu[:, width:]


def chain_barrier(me, n):
    barrier = pltpu.get_barrier_semaphore()
    for other in (lax.rem(me + 1, n), lax.rem(me + n - 1, n)):
        pl.semaphore_signal(
            barrier, inc=1, device_id={"ctx": other}, device_id_type=pl.DeviceIdType.MESH
        )
    pl.semaphore_wait(barrier, 2)


def chain(n, place, way, heads, held, out, send_sem, recv_sem, advance):
    me = lax.axis_index("ctx")
    other = lax.rem(me + way + n, n)

    @pl.when(place == 0)
    def _():
        held[...] = jnp.zeros_like(held)

    def move(h):
        return pltpu.make_async_remote_copy(
            src_ref=out.at[h],
            dst_ref=held.at[h],
            send_sem=send_sem.at[h],
            recv_sem=recv_sem.at[h],
            device_id={"ctx": other},
            device_id_type=pl.DeviceIdType.MESH,
        )

    def step(h, carry):
        @pl.when(place > 0)
        def _():
            move(h).wait_recv()

        @pl.when(place < n - 1)
        def _():
            out[h] = advance(h, held[h]).astype(BF16)
            move(h).start()

        return carry

    lax.fori_loop(0, heads, step, 0)

    @pl.when(place < n - 1)
    def _():
        def finish(h, carry):
            move(h).wait_send()
            return carry

        lax.fori_loop(0, heads, finish, 0)


def forward_kernel(n, m_ref, off_ref, qe_ref, o0_ref, s_ref, ho_ref, held, out, send_sem, recv_sem):
    heads, width = off_ref.shape[0], off_ref.shape[1]
    me = lax.axis_index("ctx")
    chain_barrier(me, n)

    def advance(h, state):
        return mm((m_ref[h, 0], m_ref[h, 1]), (state,)) + off_ref[h]

    chain(n, me, 1, heads, held, out, send_sem, recv_sem, advance)
    s_ref[...] = held[...]
    for h in range(heads):
        ho_ref[:, h * width : (h + 1) * width] = (
            mm((qe_ref[h, 0], qe_ref[h, 1]), (held[h],)) + o0_ref[h]
        ).astype(BF16)


def backward_kernel(n, m_ref, qe_ref, do_ref, d_ref, own, held, out, send_sem, recv_sem):
    heads, width = m_ref.shape[0], m_ref.shape[2]
    me = lax.axis_index("ctx")
    chain_barrier(me, n)
    for h in range(heads):
        own[h] = mm(
            (qe_ref[h, 0], qe_ref[h, 1]), halves(do_ref[:, h * width : (h + 1) * width]), TN
        )

    def advance(h, state):
        return mm((m_ref[h, 0], m_ref[h, 1]), (state,), TN) + own[h]

    chain(n, n - 1 - me, -1, heads, held, out, send_sem, recv_sem, advance)
    d_ref[...] = held[...]


def finish_kernel(group, q_ref, k_ref, v_ref, b_ref, th_ref, tl_ref, wu_ref, s_ref, d_ref, do_ref, dq_ref, dk_ref, dv_ref, db_ref):
    length, width = q_ref.shape[0], q_ref.shape[1] // group
    rows, cols = time_ids(length, 0), time_ids(length, 1)
    visible = visible_mask(length)
    below = cols < rows
    for g in range(group):
        here = slice(g * width, (g + 1) * width)
        key = stacked(k_ref, g, width).astype(F32)
        value = stacked(v_ref, g, width).astype(F32)
        query = q_ref[:, here].astype(F32)
        k_norm, q_norm = inverse_norm(key), inverse_norm(query)
        key, query = key * k_norm, query * q_norm
        b = b_ref[g]
        kp, qp = halves(key), halves(query)
        start, end_grad = (s_ref[g],), (d_ref[g],)
        gp = halves(do_ref[:, here])
        gram = mm(kp, kp, NT)
        scores = jnp.where(visible, mm(qp, kp, NT), 0.0)
        wu = wu_ref[g]
        updates = wu[:, width:] - mm(halves(wu[:, :width]), start)
        up = halves(updates)
        update_grad = mm(halves(scores), gp, TN) + mm(kp, end_grad)
        right_grad = mm((th_ref[g], tl_ref[g]), halves(update_grad), TN)
        score_grad = halves(jnp.where(visible, mm(gp, up, NT), 0.0))
        query_grad = mm(gp, start, NT) + mm(score_grad, kp)
        system_grad = jnp.where(below, -mm(halves(right_grad), up, NT), 0.0)
        residual = value - mm(kp, start)
        db_ref[g] = jnp.sum(right_grad * residual, axis=1, keepdims=True) + jnp.sum(
            system_grad * gram, axis=1, keepdims=True
        )
        gram_grad = halves(b * system_grad)
        value_grad = b * right_grad
        key_grad = (
            mm(score_grad, qp, TN)
            + mm(up, end_grad, NT)
            - mm(halves(value_grad), start, NT)
            + mm(gram_grad, kp)
            + mm(gram_grad, kp, TN)
        )
        query_grad = q_norm * (
            query_grad - query * jnp.sum(query * query_grad, axis=1, keepdims=True)
        )
        key_grad = k_norm * (key_grad - key * jnp.sum(key * key_grad, axis=1, keepdims=True))
        dq_ref[:, here] = query_grad.astype(BF16)
        for j in range(2):
            there = slice((2 * g + j) * width, (2 * g + j + 1) * width)
            dk_ref[:, there] = key_grad[j * length : (j + 1) * length].astype(BF16)
            dv_ref[:, there] = value_grad[j * length : (j + 1) * length].astype(BF16)


def per_head(group, *shape):
    return pl.BlockSpec((group,) + shape, lambda i: (i,) + (0,) * len(shape))


def per_column(group, length, width):
    return pl.BlockSpec((length, group * width), lambda i: (0, i))


def mixed_share(heads_out, weight_full):
    size = lax.axis_size("tp")
    if size != 2:
        partial = jnp.dot(heads_out, weight_full.T, preferred_element_type=F32).astype(BF16)
        return lax.psum_scatter(partial, "tp", scatter_dimension=1, tiled=True)
    half = weight_full.shape[0] // 2
    me = lax.axis_index("tp")

    def part(index):
        rows = lax.dynamic_slice_in_dim(weight_full, index * half, half, 0)
        return lax.dot_general(heads_out, rows, NT, preferred_element_type=F32)

    theirs = lax.ppermute(part(1 - me).astype(BF16), "tp", [(0, 1), (1, 0)])
    return (part(me) + theirs.astype(F32)).astype(BF16)


def local(n, queries, keys, values, beta_logit, out_weight, out_grad):
    heads = beta_logit.shape[0]
    length = queries.shape[0]
    width = queries.shape[1] // heads
    double = 2 * length
    group = 2
    tp = lax.axis_size("tp")
    anywhere = pl.BlockSpec(memory_space=pl.ANY)
    dma = pltpu.SemaphoreType.DMA
    params = pltpu.CompilerParams(vmem_limit_bytes=LIMIT)

    weight_full = lax.all_gather(out_weight, "ctx", axis=0, tiled=True)
    strength = 2.0 * jax.nn.sigmoid(beta_logit)
    gate = strength.reshape(heads, length, 2).transpose(0, 2, 1).reshape(heads, double, 1)

    shape = jax.ShapeDtypeStruct
    q_spec, k_spec = per_column(group, length, width), per_column(group, length, 2 * width)
    b_spec = per_head(group, double, 1)
    t_spec = per_head(group, double, double)
    wu_spec = per_head(group, double, 2 * width)
    inv_hi, inv_lo, wu, trans, offset, query_eff, own_out, grad_full = pl.pallas_call(
        functools.partial(swap_prepare_kernel, tp, group),
        grid=(heads // group,),
        in_specs=[q_spec, k_spec, k_spec, b_spec, anywhere],
        out_specs=[
            t_spec,
            t_spec,
            wu_spec,
            per_head(group, 2, width, width),
            per_head(group, width, width),
            per_head(group, 2, length, width),
            per_head(group, length, width),
            anywhere,
        ],
        out_shape=[
            shape((heads, double, double), BF16),
            shape((heads, double, double), BF16),
            shape((heads, double, 2 * width), F32),
            shape((heads, 2, width, width), BF16),
            shape((heads, width, width), F32),
            shape((heads, 2, length, width), BF16),
            shape((heads, length, width), F32),
            shape((length, out_grad.shape[1] * tp), BF16),
        ],
        scratch_shapes=[dma((max(tp - 1, 1),)), dma((max(tp - 1, 1),)), dma(())],
        compiler_params=pltpu.CompilerParams(
            vmem_limit_bytes=LIMIT, collective_id=2, has_side_effects=True
        ),
        name="prepare",
    )(queries, keys, values, gate, out_grad)
    grad_cols = lax.all_to_all(grad_full, "ctx", split_axis=1, concat_axis=0, tiled=True)
    trans, grad_cols = lax.optimization_barrier((trans, grad_cols))

    whole = pl.BlockSpec(memory_space=pltpu.VMEM)
    carried = [
        pltpu.VMEM((heads, width, width), BF16),
        pltpu.VMEM((heads, width, width), BF16),
        pltpu.SemaphoreType.DMA((heads,)),
        pltpu.SemaphoreType.DMA((heads,)),
    ]
    state_in, heads_out = pl.pallas_call(
        functools.partial(forward_kernel, n),
        in_specs=[whole] * 4,
        out_specs=[whole, whole],
        out_shape=[shape((heads, width, width), BF16), shape(queries.shape, BF16)],
        scratch_shapes=carried,
        compiler_params=pltpu.CompilerParams(
            vmem_limit_bytes=LIMIT, collective_id=0, has_side_effects=True
        ),
        name="forward_chain",
    )(trans, offset, query_eff, own_out)

    heads_full = lax.all_gather(heads_out, "ctx", axis=0, tiled=True)
    head_grad = jnp.dot(grad_full, weight_full, preferred_element_type=F32)

    state_grad = pl.pallas_call(
        functools.partial(backward_kernel, n),
        in_specs=[whole] * 3,
        out_specs=whole,
        out_shape=shape((heads, width, width), BF16),
        scratch_shapes=[pltpu.VMEM((heads, width, width), F32)] + carried,
        compiler_params=pltpu.CompilerParams(
            vmem_limit_bytes=LIMIT, collective_id=1, has_side_effects=True
        ),
        name="backward_chain",
    )(trans, query_eff, head_grad)

    heads_late, weight_late, _ = lax.optimization_barrier((heads_out, weight_full, state_grad))
    mixed = mixed_share(heads_late, weight_late)

    d_spec = per_head(group, width, width)
    query_grad, key_grad, value_grad, gate_grad = pl.pallas_call(
        functools.partial(finish_kernel, group),
        grid=(heads // group,),
        in_specs=[q_spec, k_spec, k_spec, b_spec, t_spec, t_spec, wu_spec, d_spec, d_spec, q_spec],
        out_specs=[q_spec, k_spec, k_spec, b_spec],
        out_shape=[
            shape(queries.shape, BF16),
            shape(keys.shape, BF16),
            shape(values.shape, BF16),
            shape((heads, double, 1), F32),
        ],
        compiler_params=params,
        name="finish",
    )(queries, keys, values, gate, inv_hi, inv_lo, wu, state_in, state_grad, head_grad)

    gate_grad = gate_grad.reshape(heads, 2, length).transpose(0, 2, 1).reshape(heads, double)
    logit_grad = gate_grad * strength * jax.nn.sigmoid(-beta_logit)

    heads_full, _, mixed = lax.optimization_barrier((heads_full, query_grad, mixed))
    scale_factor = 1.0 / math.sqrt(length * n)
    weight_grad = scale_factor * lax.dot_general(
        grad_cols, heads_full, TN, preferred_element_type=F32
    )
    return (mixed, query_grad, key_grad, value_grad, logit_grad, weight_grad)


def solution(mesh):
    placed = (
        P("ctx", "tp"),
        P("ctx", "tp"),
        P("ctx", "tp"),
        P("tp", "ctx"),
        P("ctx", "tp"),
        P("ctx", "tp"),
    )
    return jax.shard_map(
        functools.partial(local, mesh.shape["ctx"]),
        mesh=mesh,
        in_specs=placed,
        out_specs=(
            P("ctx", "tp"),
            P("ctx", "tp"),
            P("ctx", "tp"),
            P("ctx", "tp"),
            P("tp", "ctx"),
            P("ctx", "tp"),
        ),
        check_vma=False,
    )
```

```python
import functools
import math

import jax
import jax.numpy as jnp
from jax import lax
from jax.experimental import pallas as pl
from jax.experimental.pallas import tpu as pltpu
from jax.sharding import PartitionSpec as P

F32 = jnp.float32
BF16 = jnp.bfloat16
NN = (((1,), (0,)), ((), ()))
NT = (((1,), (1,)), ((), ()))
TN = (((0,), (0,)), ((), ()))
LIMIT = 56 * 1024 * 1024


def halves(x):
    high = x.astype(BF16)
    return (high, (x - high.astype(F32)).astype(BF16))


def mm(left, right, dims=NN):
    total = None
    for i, a in enumerate(left):
        for j, b in enumerate(right):
            if i + j < 2:
                term = lax.dot_general(a, b, dims, preferred_element_type=F32)
                total = term if total is None else total + term
    return total


def inverse_norm(x):
    return lax.rsqrt(jnp.sum(x * x, axis=-1, keepdims=True) + 1e-06)


def stacked(ref, head, width):
    start = head * 2 * width
    return jnp.concatenate(
        [ref[:, start : start + width], ref[:, start + width : start + 2 * width]], axis=0
    )


def time_ids(length, axis):
    ids = lax.broadcasted_iota(jnp.int32, (2 * length, 2 * length), axis)
    second = (ids >= length).astype(jnp.int32)
    return 2 * (ids - second * length) + second


def visible_mask(length):
    token = lax.broadcasted_iota(jnp.int32, (length, 2 * length), 0)
    refl = lax.broadcasted_iota(jnp.int32, (length, 2 * length), 1)
    refl = jnp.where(refl >= length, refl - length, refl)
    return refl <= token


MESH = pl.DeviceIdType.MESH


def greet(devices):
    barrier = pltpu.get_barrier_semaphore()
    for device in devices:
        pl.semaphore_signal(barrier, inc=1, device_id=device, device_id_type=MESH)
    pl.semaphore_wait(barrier, len(devices))


def columns_swap(tp, block, full, sems):
    me, cols = lax.axis_index("tp"), block.shape[1]
    sends, receives = [], []
    for d in range(1, tp):
        for kept, source in ((sends, me), (receives, lax.rem(me - d + tp, tp))):
            kept.append(
                pltpu.make_async_remote_copy(
                    src_ref=block,
                    dst_ref=full.at[:, pl.ds(pl.multiple_of(source * cols, 128), cols)],
                    send_sem=sems[0].at[d - 1],
                    recv_sem=sems[1].at[d - 1],
                    device_id={"tp": lax.rem(me + d, tp)},
                    device_id_type=MESH,
                )
            )
    own = pltpu.make_async_copy(
        block, full.at[:, pl.ds(pl.multiple_of(me * cols, 128), cols)], sems[2]
    )
    return sends, receives, own


def swap_prepare_kernel(tp, group, q_ref, k_ref, v_ref, b_ref, g_ref, th_ref, tl_ref, wu_ref, m_ref, off_ref, qe_ref, o0_ref, gf_ref, *sems):
    step, steps = pl.program_id(0), pl.num_programs(0)
    sends, receives, own = columns_swap(tp, g_ref, gf_ref, sems)

    @pl.when(step == 0)
    def _():
        own.start()
        greet([{"tp": lax.rem(lax.axis_index("tp") + d, tp)} for d in range(1, tp)])
        for copy in sends:
            copy.start()

    prepare_kernel(group, q_ref, k_ref, v_ref, b_ref, th_ref, tl_ref, wu_ref, m_ref, off_ref, qe_ref, o0_ref)

    @pl.when(step == steps - 1)
    def _():
        for sent, received in zip(sends, receives):
            sent.wait_send()
            received.wait_recv()
        own.wait()


def prepare_kernel(group, q_ref, k_ref, v_ref, b_ref, th_ref, tl_ref, wu_ref, m_ref, off_ref, qe_ref, o0_ref):
    length, width = q_ref.shape[0], q_ref.shape[1] // group
    rows, cols = time_ids(length, 0), time_ids(length, 1)
    visible = visible_mask(length)
    diff = rows ^ cols
    eye = (rows == cols).astype(F32)
    small_eye = (
        lax.broadcasted_iota(jnp.int32, (width, width), 0)
        == lax.broadcasted_iota(jnp.int32, (width, width), 1)
    ).astype(F32)
    state = []
    for g in range(group):
        key = stacked(k_ref, g, width).astype(F32)
        value = stacked(v_ref, g, width).astype(F32)
        query = q_ref[:, g * width : (g + 1) * width].astype(F32)
        key = key * inverse_norm(key)
        query = query * inverse_norm(query)
        b = b_ref[g]
        kp, qp = halves(key), halves(query)
        system = jnp.where(cols < rows, b * mm(kp, kp, NT), 0.0)
        ah, al = halves(system)
        inv = eye - jnp.where(diff == 1, system, 0.0)
        state.append([kp, qp, ah, al, inv, key, query, value, b])
    step = 2
    while step < 2 * length:
        inside = (diff >= step) & (diff < 2 * step)
        for s in state:
            part = (
                jnp.where(inside, s[2], jnp.zeros_like(s[2])),
                jnp.where(inside, s[3], jnp.zeros_like(s[3])),
            )
            ip = halves(s[4])
            s[4] = s[4] - mm(ip, halves(mm(part, ip)))
        step *= 2
    for g, (kp, qp, _, _, inv, key, query, value, b) in enumerate(state):
        ip = halves(inv)
        th_ref[g] = ip[0]
        tl_ref[g] = ip[1]
        wu = mm(ip, halves(b * jnp.concatenate([key, value], axis=1)))
        wu_ref[g] = wu
        wup = halves(wu)
        ku = mm(kp, wup, TN)
        m_hi, m_lo = halves(small_eye - ku[:, :width])
        m_ref[g, 0] = m_hi
        m_ref[g, 1] = m_lo
        off_ref[g] = ku[:, width:]
        scores = jnp.where(visible, mm(qp, kp, NT), 0.0)
        pu = mm(halves(scores), wup)
        q_hi, q_lo = halves(query - pu[:, :width])
        qe_ref[g, 0] = q_hi
        qe_ref[g, 1] = q_lo
        o0_ref[g] = pu[:, width:]


def chain_barrier(me, n):
    barrier = pltpu.get_barrier_semaphore()
    for other in (lax.rem(me + 1, n), lax.rem(me + n - 1, n)):
        pl.semaphore_signal(
            barrier, inc=1, device_id={"ctx": other}, device_id_type=pl.DeviceIdType.MESH
        )
    pl.semaphore_wait(barrier, 2)


def chain(n, place, way, heads, held, out, send_sem, recv_sem, advance):
    me = lax.axis_index("ctx")
    other = lax.rem(me + way + n, n)

    @pl.when(place == 0)
    def _():
        held[...] = jnp.zeros_like(held)

    def move(h):
        return pltpu.make_async_remote_copy(
            src_ref=out.at[h],
            dst_ref=held.at[h],
            send_sem=send_sem.at[h],
            recv_sem=recv_sem.at[h],
            device_id={"ctx": other},
            device_id_type=pl.DeviceIdType.MESH,
        )

    def step(h, carry):
        @pl.when(place > 0)
        def _():
            move(h).wait_recv()

        @pl.when(place < n - 1)
        def _():
            out[h] = advance(h, held[h]).astype(BF16)
            move(h).start()

        return carry

    lax.fori_loop(0, heads, step, 0)

    @pl.when(place < n - 1)
    def _():
        def finish(h, carry):
            move(h).wait_send()
            return carry

        lax.fori_loop(0, heads, finish, 0)


def forward_kernel(n, m_ref, off_ref, qe_ref, o0_ref, s_ref, ho_ref, held, out, send_sem, recv_sem):
    heads, width = off_ref.shape[0], off_ref.shape[1]
    me = lax.axis_index("ctx")
    chain_barrier(me, n)

    def advance(h, state):
        return mm((m_ref[h, 0], m_ref[h, 1]), (state,)) + off_ref[h]

    chain(n, me, 1, heads, held, out, send_sem, recv_sem, advance)
    s_ref[...] = held[...]
    for h in range(heads):
        ho_ref[:, h * width : (h + 1) * width] = (
            mm((qe_ref[h, 0], qe_ref[h, 1]), (held[h],)) + o0_ref[h]
        ).astype(BF16)


def backward_kernel(n, m_ref, qe_ref, do_ref, d_ref, own, held, out, send_sem, recv_sem):
    heads, width = m_ref.shape[0], m_ref.shape[2]
    me = lax.axis_index("ctx")
    chain_barrier(me, n)
    for h in range(heads):
        own[h] = mm(
            (qe_ref[h, 0], qe_ref[h, 1]), halves(do_ref[:, h * width : (h + 1) * width]), TN
        )

    def advance(h, state):
        return mm((m_ref[h, 0], m_ref[h, 1]), (state,), TN) + own[h]

    chain(n, n - 1 - me, -1, heads, held, out, send_sem, recv_sem, advance)
    d_ref[...] = held[...]


def finish_kernel(group, q_ref, k_ref, v_ref, b_ref, th_ref, tl_ref, wu_ref, s_ref, d_ref, do_ref, dq_ref, dk_ref, dv_ref, db_ref):
    length, width = q_ref.shape[0], q_ref.shape[1] // group
    rows, cols = time_ids(length, 0), time_ids(length, 1)
    visible = visible_mask(length)
    below = cols < rows
    for g in range(group):
        here = slice(g * width, (g + 1) * width)
        key = stacked(k_ref, g, width).astype(F32)
        value = stacked(v_ref, g, width).astype(F32)
        query = q_ref[:, here].astype(F32)
        k_norm, q_norm = inverse_norm(key), inverse_norm(query)
        key, query = key * k_norm, query * q_norm
        b = b_ref[g]
        kp, qp = halves(key), halves(query)
        start, end_grad = (s_ref[g],), (d_ref[g],)
        gp = halves(do_ref[:, here])
        gram = mm(kp, kp, NT)
        scores = jnp.where(visible, mm(qp, kp, NT), 0.0)
        wu = wu_ref[g]
        updates = wu[:, width:] - mm(halves(wu[:, :width]), start)
        up = halves(updates)
        update_grad = mm(halves(scores), gp, TN) + mm(kp, end_grad)
        right_grad = mm((th_ref[g], tl_ref[g]), halves(update_grad), TN)
        score_grad = halves(jnp.where(visible, mm(gp, up, NT), 0.0))
        query_grad = mm(gp, start, NT) + mm(score_grad, kp)
        system_grad = jnp.where(below, -mm(halves(right_grad), up, NT), 0.0)
        residual = value - mm(kp, start)
        db_ref[g] = jnp.sum(right_grad * residual, axis=1, keepdims=True) + jnp.sum(
            system_grad * gram, axis=1, keepdims=True
        )
        gram_grad = halves(b * system_grad)
        value_grad = b * right_grad
        key_grad = (
            mm(score_grad, qp, TN)
            + mm(up, end_grad, NT)
            - mm(halves(value_grad), start, NT)
            + mm(gram_grad, kp)
            + mm(gram_grad, kp, TN)
        )
        query_grad = q_norm * (
            query_grad - query * jnp.sum(query * query_grad, axis=1, keepdims=True)
        )
        key_grad = k_norm * (key_grad - key * jnp.sum(key * key_grad, axis=1, keepdims=True))
        dq_ref[:, here] = query_grad.astype(BF16)
        for j in range(2):
            there = slice((2 * g + j) * width, (2 * g + j + 1) * width)
            dk_ref[:, there] = key_grad[j * length : (j + 1) * length].astype(BF16)
            dv_ref[:, there] = value_grad[j * length : (j + 1) * length].astype(BF16)


def per_head(group, *shape):
    return pl.BlockSpec((group,) + shape, lambda i: (i,) + (0,) * len(shape))


def per_column(group, length, width):
    return pl.BlockSpec((length, group * width), lambda i: (0, i))


def mixed_share(heads_out, weight_full):
    size = lax.axis_size("tp")
    if size != 2:
        partial = jnp.dot(heads_out, weight_full.T, preferred_element_type=F32).astype(BF16)
        return lax.psum_scatter(partial, "tp", scatter_dimension=1, tiled=True)
    half = weight_full.shape[0] // 2
    me = lax.axis_index("tp")

    def part(index):
        rows = lax.dynamic_slice_in_dim(weight_full, index * half, half, 0)
        return lax.dot_general(heads_out, rows, NT, preferred_element_type=F32)

    theirs = lax.ppermute(part(1 - me).astype(BF16), "tp", [(0, 1), (1, 0)])
    return (part(me) + theirs.astype(F32)).astype(BF16)


def local(n, queries, keys, values, beta_logit, out_weight, out_grad):
    heads = beta_logit.shape[0]
    length = queries.shape[0]
    width = queries.shape[1] // heads
    double = 2 * length
    group = 2
    tp = lax.axis_size("tp")
    anywhere = pl.BlockSpec(memory_space=pl.ANY)
    dma = pltpu.SemaphoreType.DMA
    params = pltpu.CompilerParams(vmem_limit_bytes=LIMIT)

    weight_full = lax.all_gather(out_weight, "ctx", axis=0, tiled=True)
    strength = 2.0 * jax.nn.sigmoid(beta_logit)
    gate = strength.reshape(heads, length, 2).transpose(0, 2, 1).reshape(heads, double, 1)

    shape = jax.ShapeDtypeStruct
    q_spec, k_spec = per_column(group, length, width), per_column(group, length, 2 * width)
    b_spec = per_head(group, double, 1)
    t_spec = per_head(group, double, double)
    wu_spec = per_head(group, double, 2 * width)
    inv_hi, inv_lo, wu, trans, offset, query_eff, own_out, grad_full = pl.pallas_call(
        functools.partial(swap_prepare_kernel, tp, group),
        grid=(heads // group,),
        in_specs=[q_spec, k_spec, k_spec, b_spec, anywhere],
        out_specs=[
            t_spec,
            t_spec,
            wu_spec,
            per_head(group, 2, width, width),
            per_head(group, width, width),
            per_head(group, 2, length, width),
            per_head(group, length, width),
            anywhere,
        ],
        out_shape=[
            shape((heads, double, double), BF16),
            shape((heads, double, double), BF16),
            shape((heads, double, 2 * width), F32),
            shape((heads, 2, width, width), BF16),
            shape((heads, width, width), F32),
            shape((heads, 2, length, width), BF16),
            shape((heads, length, width), F32),
            shape((length, out_grad.shape[1] * tp), BF16),
        ],
        scratch_shapes=[dma((max(tp - 1, 1),)), dma((max(tp - 1, 1),)), dma(())],
        compiler_params=pltpu.CompilerParams(
            vmem_limit_bytes=LIMIT, collective_id=2, has_side_effects=True
        ),
        name="prepare",
    )(queries, keys, values, gate, out_grad)
    grad_cols = lax.all_to_all(grad_full, "ctx", split_axis=1, concat_axis=0, tiled=True)
    trans, grad_cols = lax.optimization_barrier((trans, grad_cols))

    whole = pl.BlockSpec(memory_space=pltpu.VMEM)
    carried = [
        pltpu.VMEM((heads, width, width), BF16),
        pltpu.VMEM((heads, width, width), BF16),
        pltpu.SemaphoreType.DMA((heads,)),
        pltpu.SemaphoreType.DMA((heads,)),
    ]
    state_in, heads_out = pl.pallas_call(
        functools.partial(forward_kernel, n),
        in_specs=[whole] * 4,
        out_specs=[whole, whole],
        out_shape=[shape((heads, width, width), BF16), shape(queries.shape, BF16)],
        scratch_shapes=carried,
        compiler_params=pltpu.CompilerParams(
            vmem_limit_bytes=LIMIT, collective_id=0, has_side_effects=True
        ),
        name="forward_chain",
    )(trans, offset, query_eff, own_out)

    head_grad = jnp.dot(grad_full, weight_full, preferred_element_type=F32)

    state_grad = pl.pallas_call(
        functools.partial(backward_kernel, n),
        in_specs=[whole] * 3,
        out_specs=whole,
        out_shape=shape((heads, width, width), BF16),
        scratch_shapes=[pltpu.VMEM((heads, width, width), F32)] + carried,
        compiler_params=pltpu.CompilerParams(
            vmem_limit_bytes=LIMIT, collective_id=1, has_side_effects=True
        ),
        name="backward_chain",
    )(trans, query_eff, head_grad)

    heads_late, weight_late, state_grad = lax.optimization_barrier(
        (heads_out, weight_full, state_grad)
    )
    heads_full = lax.all_gather(heads_late, "ctx", axis=0, tiled=True)
    mixed = mixed_share(heads_late, weight_late)

    d_spec = per_head(group, width, width)
    query_grad, key_grad, value_grad, gate_grad = pl.pallas_call(
        functools.partial(finish_kernel, group),
        grid=(heads // group,),
        in_specs=[q_spec, k_spec, k_spec, b_spec, t_spec, t_spec, wu_spec, d_spec, d_spec, q_spec],
        out_specs=[q_spec, k_spec, k_spec, b_spec],
        out_shape=[
            shape(queries.shape, BF16),
            shape(keys.shape, BF16),
            shape(values.shape, BF16),
            shape((heads, double, 1), F32),
        ],
        compiler_params=params,
        name="finish",
    )(queries, keys, values, gate, inv_hi, inv_lo, wu, state_in, state_grad, head_grad)

    gate_grad = gate_grad.reshape(heads, 2, length).transpose(0, 2, 1).reshape(heads, double)
    logit_grad = gate_grad * strength * jax.nn.sigmoid(-beta_logit)

    heads_full, _, mixed = lax.optimization_barrier((heads_full, query_grad, mixed))
    scale_factor = 1.0 / math.sqrt(length * n)
    weight_grad = scale_factor * lax.dot_general(
        grad_cols, heads_full, TN, preferred_element_type=F32
    )
    return (mixed, query_grad, key_grad, value_grad, logit_grad, weight_grad)


def solution(mesh):
    placed = (
        P("ctx", "tp"),
        P("ctx", "tp"),
        P("ctx", "tp"),
        P("tp", "ctx"),
        P("ctx", "tp"),
        P("ctx", "tp"),
    )
    return jax.shard_map(
        functools.partial(local, mesh.shape["ctx"]),
        mesh=mesh,
        in_specs=placed,
        out_specs=(
            P("ctx", "tp"),
            P("ctx", "tp"),
            P("ctx", "tp"),
            P("ctx", "tp"),
            P("tp", "ctx"),
            P("ctx", "tp"),
        ),
        check_vma=False,
    )
```
